32 devices in a mesh: dev: 32 (over z, y, x, core).
Axes of the slice: x: 2, y: 2, z: 4, core: 2. Of those that a mesh axis runs over, the one named last changes fastest.
Arguments:
- states: float32 [188, 262144], P(None, 'dev'), may hold values from -6 to 6
- particle_mass: float32 [262144], P('dev'), may hold values from 1 to 10
- bin_index: int32 [262144], P('dev'), may hold values from 0 to 3
- cell_index: int32 [262144], P('dev'), may hold values from 0 to 255, as said below
- move_slot: int32 [262144], P('dev'), may hold values from -1 to 1023, as said below
- react_list: int32 [65536], P('dev'), may hold values from -1 to 8191, as said below
- rate_weights: bfloat16 [939, 188], replicated, may hold values from -0.4375 to 0.4375
- stoichiometry: bfloat16 [188, 939], replicated, may hold values from -0.1875 to 0.1875
- rate_scale: float32 [939], replicated, may hold values from 0.2 to 2
- jacobian_inverse: bfloat16 [4, 188, 188], replicated, may hold values from -1 to 2
- mixing_rate: float32 [8192], P('dev'), may hold values from 0.5 to 8
Outputs:
- mixed_states: float32 [188, 294912], P(None, 'dev')
- cell_means: float32 [188, 8192], P(None, 'dev')
The draws below stay inside these ranges and needn't reach their ends.
Inputs may be any that keep to these rules, and one draw needn't show every extreme that they name: `move_slot`: on each device the entries that are not -1 are distinct. Entries below 512 never stand on device 0 and entries of 512 or more never on the last device. At most 512 particles of one device go each way, and that many go down from some device and up from some device. Every cell of every device keeps at least one staying particle. `cell_index`: for a staying particle, its cell on its own device; for a moving one, its cell on the device it moves to. `react_list`: each device lists distinct particles of its own first, then -1. A quarter of the devices list 2048 particles, the others 2048 // 4.
All inputs are finite; a program needn't handle non-finite values.
Results may differ from the reference program's by a relative error of at most 0.00089.
Values sent between devices are 32-bit elements; how exact they have to be, the bound alone decides.
A program may use at most 128 MiB of HBM per device.

```python
import math
import jax
import jax.numpy as jnp
from jax import lax

S = 188
R = 939
NB = 4
NEWTON = 3
P_DEV = 8192
MCAP = 512
C_DEV = 256
R_MAX = 2048
HELP_DEV = 896
NLOC = 9216
PARTICLES = 262144
CELLS = 8192
N_DEV = 32


def chemistry_lists(key):
    base = jax.random.fold_in(key, 7)
    heavy = jax.random.permutation(jax.random.fold_in(base, 1), N_DEV) < N_DEV // 4
    counts = jnp.where(heavy, R_MAX, R_MAX // 4).astype(jnp.int32)
    device_ids = jnp.arange(N_DEV, dtype=jnp.int32)

    def shuffled(device):
        return jax.random.permutation(jax.random.fold_in(jax.random.fold_in(base, 2), device), P_DEV)[:R_MAX]
    chosen = jax.vmap(shuffled)(device_ids).astype(jnp.int32)
    entry = jnp.arange(R_MAX, dtype=jnp.int32)[None, :]
    filled = entry < counts[:, None]
    react = jnp.where(filled, chosen, -1).astype(jnp.int32)
    return react.reshape(-1)


def migration_lists(key):
    base = jax.random.fold_in(key, 13)
    device_ids = jnp.arange(N_DEV, dtype=jnp.int32)
    dropped = jax.random.randint(jax.random.fold_in(base, 1), (N_DEV, 2), 0, MCAP // 2 + 1)
    pick_lower = jax.random.randint(jax.random.fold_in(base, 2), (), 1, N_DEV)
    pick_upper = jax.random.randint(jax.random.fold_in(base, 3), (), 0, N_DEV - 1)
    downward = jnp.where(device_ids == pick_lower, MCAP, MCAP - dropped[:, 0])
    downward = jnp.where(device_ids == 0, 0, downward)
    upward = jnp.where(device_ids == pick_upper, MCAP, MCAP - dropped[:, 1])
    upward = jnp.where(device_ids == N_DEV - 1, 0, upward)

    def one_device(device, down_count, up_count):
        dkey = jax.random.fold_in(jax.random.fold_in(base, 4), device)
        shuffled = jax.random.permutation(jax.random.fold_in(dkey, 1), P_DEV).astype(jnp.int32)
        place = jnp.arange(P_DEV, dtype=jnp.int32)
        values = jnp.where(place < down_count, place, jnp.where(place < down_count + up_count, MCAP + place - down_count, -1))
        stay_rank = place - down_count - up_count
        random_cells = jax.random.randint(jax.random.fold_in(dkey, 2), (P_DEV,), 0, C_DEV)
        cells = jnp.where((stay_rank >= 0) & (stay_rank < C_DEV), stay_rank, random_cells)
        slot_out = jnp.zeros((P_DEV,), jnp.int32).at[shuffled].set(values.astype(jnp.int32))
        cell_out = jnp.zeros((P_DEV,), jnp.int32).at[shuffled].set(cells.astype(jnp.int32))
        return (slot_out, cell_out)
    slot_all, cell_all = jax.vmap(one_device)(device_ids, downward, upward)
    return (slot_all.reshape(-1), cell_all.reshape(-1))


def draw_react_list(key, part):
    return chemistry_lists(key)


def draw_move_slot(key, part):
    return migration_lists(key)[0]


def draw_cell_index(key, part):
    return migration_lists(key)[1]


def draw_jacobian_inverse(key, part):
    noise = jax.random.truncated_normal(key, -4.0, 4.0, (NB, S, S), jnp.float32)
    identity = jnp.eye(S, dtype=jnp.float32)[None, :, :]
    return (identity + 0.3 / math.sqrt(S) * noise).astype(jnp.bfloat16)


def place_ends(drawn, key, low, largest):
    longest = drawn.shape.index(max(drawn.shape))
    spots = []
    for shift in (0, 1):
        where = [jax.random.randint(jax.random.fold_in(key, axis), (), 0, length) for axis, length in enumerate(drawn.shape)]
        where[longest] = (where[longest] + shift) % drawn.shape[longest]
        spots.append(tuple(where))
    return drawn.at[spots[0]].set(low).at[spots[1]].set(largest)


def block_levels(rng, extent, shards, smallest, top_value):
    level, own = 1.0, jax.random.fold_in(rng, 6)
    for position, shards_of in shards:
        heights = jnp.exp(jax.random.uniform(jax.random.fold_in(own, position), (shards_of,), jnp.float32, smallest / len(shards), top_value / len(shards)))
        level = level * jnp.repeat(heights, extent[position] // shards_of).reshape([-1 if axis == position else 1 for axis in range(len(extent))])
    return level


def centred(rng, shape, scale, most, split=(), kind=jnp.bfloat16):
    loudness = block_levels(rng, shape, split, -0.22, 0.18) if split else 1.0
    entries = jax.random.normal(rng, shape, jnp.float32) * scale * loudness
    return jnp.minimum(jnp.maximum(entries, -most), most).astype(kind)


def setup_inputs(seed: int = 0) -> dict:
    arg_keys = jax.random.split(jax.random.key(seed), 12)
    return {
        "states": centred(arg_keys[0], (S, PARTICLES), 1.0, 6.0, ((1, 32),), jnp.float32),
        "particle_mass": jnp.clip(jnp.exp(math.log(10.0) - 2.3025851 * jax.random.uniform(arg_keys[1], (PARTICLES,), jnp.float32) ** block_levels(arg_keys[1], (PARTICLES,), ((0, 32),), -0.2, 0.2)), 1.0, 10.0),
        "bin_index": place_ends(jax.random.randint(arg_keys[2], (PARTICLES,), 0, NB), jax.random.fold_in(arg_keys[2], 1), 0, NB - 1).astype(jnp.int32),
        "cell_index": draw_cell_index(jax.random.fold_in(arg_keys[11], 71), 0),
        "move_slot": draw_move_slot(jax.random.fold_in(arg_keys[11], 71), 0),
        "react_list": draw_react_list(jax.random.fold_in(arg_keys[11], 71), 0),
        "rate_weights": centred(arg_keys[6], (R, S), S ** -0.5, 0.4375),
        "stoichiometry": centred(arg_keys[7], (S, R), R ** -0.5, 0.1875),
        "rate_scale": jnp.clip(jnp.exp(jax.random.uniform(arg_keys[8], (R,), jnp.float32, math.log(0.2), math.log(2.0))), 0.2, 2.0),
        "jacobian_inverse": draw_jacobian_inverse(jax.random.fold_in(arg_keys[11], 71), 0),
        "mixing_rate": jnp.clip(jnp.exp(math.log(8.0) - 2.7725887 * jax.random.uniform(arg_keys[10], (CELLS,), jnp.float32) ** block_levels(arg_keys[10], (CELLS,), ((0, 32),), -0.2, 0.2)), 0.5, 8.0),
    }


CHEM_STEP = 0.5
MIX_RATE = 0.5
EXACTLY = lax.Precision.HIGHEST


def newton(start, bin_mask, rate_weights, stoichiometry, rate_scale, jacobian_inverse):
    iterate = start
    mask_half = bin_mask.astype(jnp.bfloat16)
    for sweep in range(NEWTON):
        exponent = jnp.dot(rate_weights, iterate.astype(jnp.bfloat16), preferred_element_type=jnp.float32)
        reaction_rates = (rate_scale[:, None] * jax.nn.softplus(exponent)).astype(jnp.bfloat16)
        source_terms = jnp.dot(stoichiometry, reaction_rates, preferred_element_type=jnp.float32)
        residual = (iterate - start - CHEM_STEP * source_terms).astype(jnp.bfloat16)
        update = jnp.zeros_like(iterate)
        for level in range(NB):
            update = update + jnp.dot(jacobian_inverse[level], residual * mask_half[level], preferred_element_type=jnp.float32)
        iterate = iterate - update
    return iterate


def bin_table(bins):
    return (bins[None, :] == jnp.arange(NB, dtype=jnp.int32)[:, None]).astype(jnp.float32)


def cell_table(cells):
    return (cells[:, None] == jnp.arange(C_DEV, dtype=jnp.float32)[None, :]).astype(jnp.float32)


def spread(table, onehot):
    return lax.dot_general(table, onehot, (((1,), (1,)), ((), ())), precision=EXACTLY)


def mix_device(local, weights, cells, rates_dev):
    onehot = cell_table(cells)
    weighted = jnp.dot(local * weights[None, :], onehot, precision=EXACTLY)
    total = jnp.dot(weights[None, :], onehot, precision=EXACTLY)
    means = weighted / total
    factor = 1.0 - jnp.exp(-MIX_RATE * rates_dev)
    table = jnp.concatenate([means, factor[None, :]], axis=0)
    pulled = spread(table, onehot)
    mixed = local + (pulled[:-1] - local) * pulled[-1:]
    return jnp.where(weights[None, :] > 0, mixed, 0.0), means


def outgoing(device_states, masses, cells, slots):
    meta = jnp.stack([masses, cells.astype(jnp.float32)])
    to_lower = jnp.where((slots >= 0) & (slots < MCAP), slots, MCAP)
    to_upper = jnp.where(slots >= MCAP, slots - MCAP, MCAP)
    lower = jnp.zeros((S, MCAP), jnp.float32).at[:, to_lower].set(device_states, mode="drop")
    lower_meta = jnp.zeros((2, MCAP), jnp.float32).at[:, to_lower].set(meta, mode="drop")
    upper = jnp.zeros((S, MCAP), jnp.float32).at[:, to_upper].set(device_states, mode="drop")
    upper_meta = jnp.zeros((2, MCAP), jnp.float32).at[:, to_upper].set(meta, mode="drop")
    return lower, lower_meta, upper, upper_meta


def reference(states, particle_mass, bin_index, cell_index, move_slot, react_list, rate_weights, stoichiometry, rate_scale, jacobian_inverse, mixing_rate):
    live = react_list >= 0
    picked = jnp.nonzero(live, size=N_DEV * HELP_DEV)[0].astype(jnp.int32)
    columns = ((picked // R_MAX) * P_DEV + react_list[picked]).astype(jnp.int32)
    blocks = columns.reshape(N_DEV, HELP_DEV)

    def solve_block(block):
        start = jnp.take(states, block, axis=1)
        return newton(start, bin_table(jnp.take(bin_index, block)), rate_weights, stoichiometry, rate_scale, jacobian_inverse)

    solved = lax.map(solve_block, blocks)
    solved = jnp.transpose(solved, (1, 0, 2)).reshape(S, N_DEV * HELP_DEV)
    reacted = states.at[:, columns].set(solved)
    lower, lower_meta, upper, upper_meta = jax.vmap(outgoing, in_axes=(1, 0, 0, 0))(
        reacted.reshape(S, N_DEV, P_DEV), particle_mass.reshape(N_DEV, P_DEV),
        cell_index.reshape(N_DEV, P_DEV), move_slot.reshape(N_DEV, P_DEV))
    from_below = jnp.concatenate([jnp.zeros_like(upper[:1]), upper[:-1]], axis=0)
    below_meta = jnp.concatenate([jnp.zeros_like(upper_meta[:1]), upper_meta[:-1]], axis=0)
    from_above = jnp.concatenate([lower[1:], jnp.zeros_like(lower[:1])], axis=0)
    above_meta = jnp.concatenate([lower_meta[1:], jnp.zeros_like(lower_meta[:1])], axis=0)

    def mix_one(device):
        offset = (device * P_DEV).astype(jnp.int32)
        own = lax.dynamic_slice_in_dim(reacted, offset, P_DEV, 1)
        slots = lax.dynamic_slice_in_dim(move_slot, offset, P_DEV, 0)
        masses = lax.dynamic_slice_in_dim(particle_mass, offset, P_DEV, 0)
        cells = lax.dynamic_slice_in_dim(cell_index, offset, P_DEV, 0)
        rates_dev = lax.dynamic_slice_in_dim(mixing_rate, (device * C_DEV).astype(jnp.int32), C_DEV, 0)
        local = jnp.concatenate([own, from_below[device], from_above[device]], axis=1)
        weights = jnp.concatenate([jnp.where(slots < 0, masses, 0.0), below_meta[device][0], above_meta[device][0]])
        places = jnp.concatenate([cells.astype(jnp.float32), below_meta[device][1], above_meta[device][1]])
        return mix_device(local, weights, places, rates_dev)

    mixed, means = lax.map(mix_one, jnp.arange(N_DEV, dtype=jnp.int32))
    mixed_states = jnp.transpose(mixed, (1, 0, 2)).reshape(S, N_DEV * NLOC)
    cell_means = jnp.transpose(means, (1, 0, 2)).reshape(S, N_DEV * C_DEV)
    return mixed_states, cell_means
```

```python
import functools
import math
import jax
import jax.numpy as jnp
from jax import lax
from jax.experimental import pallas as pl
from jax.experimental.pallas import tpu as pltpu
from jax.sharding import PartitionSpec as P

NEWTON = 3
CHEM_STEP = 0.5
MIX_RATE = 0.5
LANES = 128
SUB = 512
SUBS = 2
NCOL = SUB * SUBS
CHUNK = 256
LAG = 2
ROWS = 192
UNROLL = 8
LOADS = 4
F32, BF16, I32 = jnp.float32, jnp.bfloat16, jnp.int32


def nt(a, b):
    return lax.dot_general(a, b, (((1,), (1,)), ((), ())), preferred_element_type=F32)


def nn(a, b):
    return jnp.dot(a, b, preferred_element_type=F32)


def iota(shape, dim):
    return lax.broadcasted_iota(I32, shape, dim)


def halves(x):
    hi = x.astype(BF16)
    return hi, (x - hi.astype(F32)).astype(BF16)


def hot(row, size):
    return (iota((size, row.shape[1]), 0) == row).astype(F32).astype(BF16)


def small_hot(row, size):
    which = iota((size, row.shape[1]), 0).astype(F32).astype(BF16)
    return jnp.where(which == row.astype(F32).astype(BF16), BF16(1), BF16(0))


def take(x, index):
    return jnp.take_along_axis(x, index, axis=1, mode="promise_in_bounds")


def tile_at(t, count=1):
    return pl.ds(pl.multiple_of(t * LANES, LANES), count * LANES)


def ranks(mask):
    tiles = mask.shape[0]
    upper_tri = (iota((LANES, LANES), 0) < iota((LANES, LANES), 1)).astype(F32).astype(BF16)
    lower_tri = (iota((tiles, tiles), 1) < iota((tiles, tiles), 0)).astype(F32).astype(BF16)
    half = mask.astype(BF16)
    before = jnp.sum(nn(lower_tri, half), axis=1, keepdims=True)
    return (nn(half, upper_tri) + before).astype(I32), before


def total_of(x):
    return jnp.sum(jnp.sum(x, axis=1, keepdims=True), axis=0, keepdims=True)


def react_kernel(
    states, mass, bins, cells, slots, rlist, rate_wt, stoich, scale_row, jac3,
    lower, upper, rank, base_v, solved,
    base_s, st, tail, index, low_rank, jac, rate_w, stoich_w, scale, packed, stack, sem, load_sems,
):
    species, count = states.shape
    tiles = count // LANES
    half = lower.shape[1]
    moved_tiles = 2 * half // LANES
    most = rlist.shape[1]
    groups = ROWS // 8
    part = count // LOADS
    loads = [
        pltpu.make_async_copy(
            states.at[:, pl.ds(i * part, part)], st.at[:, pl.ds(i * part, part)], load_sems.at[i]
        )
        for i in range(LOADS)
    ]
    for load in loads:
        load.start()

    r = rlist[...]
    listed = nt(hot(r >> 7, tiles), hot(r & 127, LANES))
    total = total_of(listed)
    moving = (slots[...] >= 0).astype(F32)
    total_move = total_of(moving)
    place, before = ranks(listed)
    place_move, before_move = ranks(moving)
    rank[...] = jnp.where(listed > 0, place, -1)
    lane = iota((tiles, LANES), 1)
    row = iota((tiles, LANES), 0)
    table = jnp.where(lane == 0, before, jnp.where(lane == 1, total, jnp.where(lane == 2, total_move, before_move)))
    for q in range(moved_tiles + 1):
        first = jnp.where((moving > 0) & (place_move == q * LANES), place.astype(F32) - total, 0.0)
        table = jnp.where((lane == 4) & (row == q), total_of(first) + total, table)
    base_v[...] = table.astype(I32)
    copy = pltpu.make_async_copy(base_v, base_s, sem)
    copy.start()
    low_rank[0] = jnp.where(listed > 0, place & 127, -1)
    low_rank[1] = jnp.where(moving > 0, place_move & 127, -1)

    scale[...] = jnp.transpose(jnp.broadcast_to(scale_row[...] * math.log(2.0), (LANES, scale_row.shape[1])))
    rate_w[...] = jnp.zeros_like(rate_w)
    rate_w[:, 0:species] = jnp.transpose(rate_wt[...].astype(F32)).astype(BF16)
    stoich_w[...] = jnp.zeros_like(stoich_w)
    stoich_w[0:species, :] = stoich[...]
    jac[...] = jnp.zeros_like(jac)
    for b in range(jac3.shape[1]):
        jac[0:species, b * ROWS : b * ROWS + species] = jac3[:, b, :]

    lanes8 = iota((8, LANES), 1).astype(F32).astype(BF16)

    def inverses(k, c):
        for u in range(UNROLL):
            t = k * UNROLL + u
            onehots = jnp.concatenate([small_hot(low_rank[s, pl.ds(t, 1), :], LANES) for s in range(2)], axis=0)
            at = pl.ds(pl.multiple_of(t * 8, 8), 8)
            index[at, :] = nt(lanes8, onehots).astype(I32)
        return c

    lax.fori_loop(0, tiles // UNROLL, inverses, 0)
    copy.wait()
    for load in loads:
        load.wait()
    rest = species - (groups - 1) * 8
    for t in range(tiles):
        at = slice(t * LANES, (t + 1) * LANES)
        rows = [mass[t : t + 1, :], (cells[t : t + 1, :] + 256 * bins[t : t + 1, :]).astype(F32),
                slots[t : t + 1, :].astype(F32), rank[t : t + 1, :].astype(F32)]
        tail[0:rest, at] = st[(groups - 1) * 8 : species, at]
        for i, value in enumerate(rows):
            tail[rest + i : rest + i + 1, at] = value

    lane8 = iota((8, LANES), 1)

    def source(g, t):
        if g == groups - 1:
            return tail[:, tile_at(t)]
        return st[8 * g : 8 * g + 8, tile_at(t)]

    def compact(out, column, which, total_at):
        def some(k, carry):
            for u in range(UNROLL):
                t = k * UNROLL + u
                first = base_s[t, column]
                after = jnp.where(t == tiles - 1, base_s[0, total_at], base_s[jnp.minimum(t + 1, tiles - 1), column])
                wraps = (after >> 7) != (first >> 7)
                inside = lane8 >= (first & 127)
                picks = index[pl.ds(pl.multiple_of(t * 8, 8), 8), which * LANES : (which + 1) * LANES]
                at = tile_at(first >> 7)
                fresh = []
                for g in range(groups):
                    got = take(source(g, t), picks)
                    new = jnp.where(inside, got, carry[g])
                    out[8 * g : 8 * g + 8, at] = new
                    fresh.append(jnp.where(wraps, got, new))
                carry = tuple(fresh)
            return carry

        carry = lax.fori_loop(
            0, tiles // UNROLL, some, tuple(jnp.zeros((8, LANES), F32) for _ in range(groups))
        )
        at = tile_at(base_s[0, total_at] >> 7)
        for g in range(groups):
            out[8 * g : 8 * g + 8, at] = carry[g]

    compact(solved, 0, 0, 1)
    compact(packed, 3, 1, 2)

    reactions = rate_w.shape[0]
    chunks = [(lo, min(CHUNK, reactions - lo)) for lo in range(0, reactions, CHUNK)]
    log2e = math.log2(math.e)

    def solve(k, c):
        subs = []
        for s in range(SUBS):
            at = pl.ds(pl.multiple_of((k * SUBS + s) * SUB, SUB), SUB)
            level = (solved[species + 1 : species + 2, at].astype(I32) >> 8).astype(F32)
            subs.append({"at": at, "start": solved[:, at], "level": level, "d": None})
        waiting = []

        def finish():
            sub, i, u = waiting.pop(0)
            lo, size = chunks[i]
            u = u * log2e
            soft = jnp.maximum(u, jnp.log2(1.0 + jnp.exp2(jnp.minimum(u, 126.0))))
            rate = (soft * scale[lo : lo + size, 0:1]).astype(BF16)
            term = nn(stoich_w[:, lo : lo + size], rate)
            sub["source"] = term if i == 0 else sub["source"] + term
            if i == len(chunks) - 1:
                d = sub["d"]
                residual = -CHEM_STEP * sub["source"]
                residual = (residual if d is None else d + residual).astype(BF16)
                masked = jnp.concatenate(
                    [jnp.where(sub["level"] == b, residual, BF16(0)) for b in range(jac3.shape[1])], axis=0
                )
                update = nn(jac[...], masked)
                sub["d"] = -update if d is None else d - update

        for sweep in range(NEWTON):
            for sub in subs:
                x = None
                for i, (lo, size) in enumerate(chunks):
                    if x is None:
                        x = (sub["start"] if sub["d"] is None else sub["start"] + sub["d"]).astype(BF16)
                    waiting.append((sub, i, nn(rate_w[lo : lo + size, :], x)))
                    if len(waiting) > LAG:
                        finish()
        while waiting:
            finish()
        for sub in subs:
            solved[:, sub["at"]] = sub["start"] + sub["d"]
        return c

    lax.fori_loop(0, (base_s[0, 1] + NCOL - 1) // NCOL, solve, 0)

    spans = []
    for q in range(moved_tiles):
        low, high = base_s[q, 4], base_s[q + 1, 4]
        spans.append((low >> 7, ((high - 1) >> 7) - (low >> 7) + 1))
    longest = functools.reduce(jnp.maximum, [s[1] for s in spans])
    final = most // LANES - 1

    def expand(s, c):
        for q in range(moved_tiles):
            here = slice(q * LANES, (q + 1) * LANES)
            t = jnp.minimum(spans[q][0] + s, final)
            wanted = packed[ROWS - 1 : ROWS, here].astype(I32)
            wanted = jnp.broadcast_to(jnp.where(lane8[0:1] + q * LANES < base_s[0, 2], wanted, -1), (8, LANES))
            mine = (wanted >> 7) == t
            picks = wanted & 127
            for g in range(groups):
                rows = slice(8 * g, 8 * g + 8)
                keep = mine if g < groups - 1 else mine & (iota((8, LANES), 0) < rest)
                packed[rows, here] = jnp.where(keep, take(solved[rows, tile_at(t)], picks), packed[rows, here])
        return c

    lax.fori_loop(0, longest, expand, 0)

    mine = packed[:, 0 : 2 * half]
    filled = iota((1, 2 * half), 1) < base_s[0, 2]
    mine = jnp.where(filled, mine, 0.0)
    hi, lo = halves(mine)
    stack[0:ROWS, :] = hi
    stack[ROWS:, :] = lo
    slot = jnp.where(filled, mine[species + 2 : species + 3].astype(I32), -1)
    for out, first in ((lower, 0), (upper, half)):
        moved = nt(stack[...], hot_rows(slot - first, half))
        out[...] = moved[0:ROWS] + moved[ROWS:]


def hot_rows(row, size):
    return (iota((size, row.shape[1]), 0) == row).astype(F32).astype(BF16)


def cell_sums(x, w, cell, n_cells):
    hi, lo = halves(x * w)
    onehot = small_hot(cell, n_cells)
    return nt(jnp.concatenate([hi, lo], axis=0), onehot)


def with_ones(x):
    width = x.shape[1]
    return jnp.concatenate([x, jnp.ones((1, width), F32), jnp.zeros((ROWS - x.shape[0] - 1, width), F32)], axis=0)


def sums_kernel(base, states, rank, solved, mass, cells, slots, reacted, sums):
    species, width = states.shape
    groups = ROWS // 8
    step = pl.program_id(0)
    lane8 = iota((8, LANES), 1)

    for b in range(width // LANES):
        here = slice(b * LANES, (b + 1) * LANES)
        first = base[step * (width // LANES) + b, 0]
        t = first >> 7
        inside = lane8 >= (first & 127)
        wanted = jnp.broadcast_to(rank[b : b + 1, :], (8, LANES))
        picks = wanted & 127
        mine = wanted >= 0
        for g in range(groups):
            n = min(8, species - 8 * g)
            rows = slice(8 * g, 8 * g + n)
            pair = jnp.where(inside[:n], solved[rows, tile_at(t)], solved[rows, tile_at(t + 1)])
            reacted[rows, here] = jnp.where(mine[:n], take(pair, picks[:n]), states[rows, here])
    w = jnp.where(slots[...] < 0, mass[...], 0.0)
    term = cell_sums(with_ones(reacted[...]), w, cells[...], sums.shape[1])

    @pl.when(step == 0)
    def _():
        sums[...] = term

    @pl.when(step > 0)
    def _():
        sums[...] += term


def arrival(ref, species):
    w = ref[species : species + 1, :]
    cell = ref[species + 1 : species + 2, :].astype(I32) & 255
    return ref[0:species, :], w, jnp.where(w > 0, cell, -1)


def mix_kernel(reacted, cells, slots, below, above, sums, mixing, mixed, means, table):
    species = reacted.shape[0]
    n_cells = sums.shape[1]
    step = pl.program_id(0)
    last = pl.num_programs(0) - 1

    @pl.when(step == 0)
    def _():
        acc = sums[...]
        for ref in (below, above):
            x, w, cell = arrival(ref, species)
            acc = acc + cell_sums(with_ones(x), w, cell, n_cells)
        acc = acc[0:ROWS] + acc[ROWS:]
        mean = acc[0:species] / acc[species : species + 1]
        means[...] = mean
        keep = jnp.exp(-MIX_RATE * mixing[...])
        table[...] = jnp.zeros_like(table)
        hi, lo = halves(mean * (1.0 - keep))
        table[0:species, 0:n_cells] = hi
        table[0:species, n_cells:] = lo
        hi, lo = halves(jnp.broadcast_to(keep, (16, n_cells)))
        table[ROWS:, 0:n_cells] = hi
        table[ROWS:, n_cells:] = lo

    def blend(x, cell):
        onehot = small_hot(cell, n_cells)
        pulled = nn(table[...], jnp.concatenate([onehot, onehot], axis=0))
        return x * pulled[ROWS : ROWS + 1] + pulled[:species]

    @pl.when(step < last)
    def _():
        mixed[...] = blend(reacted[...], jnp.where(slots[...] < 0, cells[...], -1))

    @pl.when(step == last)
    def _():
        half = below.shape[1]
        for ref, at in ((below, slice(0, half)), (above, slice(half, 2 * half))):
            x, _, cell = arrival(ref, species)
            mixed[:, at] = blend(x, cell)


def body(
    states, particle_mass, bin_index, cell_index, move_slot, react_list,
    rate_weights, stoichiometry, rate_scale, jacobian_inverse, mixing_rate, slot_count,
):
    species, count = states.shape
    n_cells = mixing_rate.shape[0]
    listed = react_list.shape[0]
    reactions = rate_scale.shape[0]
    n_bins = jacobian_inverse.shape[0]
    tiles = count // LANES
    wide = listed + 2 * LANES
    half = slot_count // 2
    square = lambda a: a.reshape(tiles, LANES)
    line = lambda a: a.reshape(1, -1)
    vmem = pl.BlockSpec(memory_space=pltpu.VMEM)
    lower, upper, rank, base, solved = pl.pallas_call(
        react_kernel,
        in_specs=[pl.BlockSpec(memory_space=pl.ANY)] + [vmem] * 9,
        out_shape=(
            jax.ShapeDtypeStruct((ROWS, half), F32),
            jax.ShapeDtypeStruct((ROWS, half), F32),
            jax.ShapeDtypeStruct((tiles, LANES), I32),
            jax.ShapeDtypeStruct((tiles, LANES), I32),
            jax.ShapeDtypeStruct((ROWS, wide), F32),
        ),
        scratch_shapes=[
            pltpu.SMEM((tiles, LANES), I32),
            pltpu.VMEM((species, count), F32),
            pltpu.VMEM((8, count), F32),
            pltpu.VMEM((tiles * 8, 2 * LANES), I32),
            pltpu.VMEM((2, tiles, LANES), I32),
            pltpu.VMEM((ROWS, n_bins * ROWS), BF16),
            pltpu.VMEM((reactions, ROWS), BF16),
            pltpu.VMEM((ROWS, reactions), BF16),
            pltpu.VMEM((reactions, LANES), F32),
            pltpu.VMEM((ROWS, slot_count + 2 * LANES), F32),
            pltpu.VMEM((2 * ROWS, slot_count), BF16),
            pltpu.SemaphoreType.DMA,
            pltpu.SemaphoreType.DMA((LOADS,)),
        ],
        compiler_params=pltpu.CompilerParams(vmem_limit_bytes=40 * 2**20),
        name="react",
    )(
        states, square(particle_mass), square(bin_index), square(cell_index), square(move_slot),
        line(react_list), rate_weights.T, stoichiometry, line(rate_scale), jnp.transpose(jacobian_inverse, (1, 0, 2)),
    )
    devices = lax.axis_size("dev")
    below = lax.ppermute(upper, "dev", [(i, i + 1) for i in range(devices - 1)])
    above = lax.ppermute(lower, "dev", [(i + 1, i) for i in range(devices - 1)])
    width = slot_count
    steps = count // width
    own = lambda rows: pl.BlockSpec((rows, width), lambda i: (0, jnp.minimum(i, steps - 1)))
    whole = lambda shape: pl.BlockSpec(shape, lambda i: (0, 0))
    masses, cell_line, slot_line = line(particle_mass), line(cell_index), line(move_slot)
    reacted, sums = pl.pallas_call(
        sums_kernel,
        grid=(steps,),
        in_specs=[
            pl.BlockSpec(memory_space=pltpu.SMEM), own(species),
            pl.BlockSpec((width // LANES, LANES), lambda i: (i, 0)),
            whole((ROWS, wide)), own(1), own(1), own(1),
        ],
        out_specs=(own(species), whole((2 * ROWS, n_cells))),
        out_shape=(jax.ShapeDtypeStruct((species, count), F32), jax.ShapeDtypeStruct((2 * ROWS, n_cells), F32)),
        compiler_params=pltpu.CompilerParams(vmem_limit_bytes=32 * 2**20),
        cost_estimate=pl.CostEstimate(
            flops=4 * ROWS * count * n_cells, bytes_accessed=8 * species * count, transcendentals=0
        ),
        name="sums",
    )(base, states, rank, solved, masses, cell_line, slot_line)
    mixed, means = pl.pallas_call(
        mix_kernel,
        grid=(steps + 1,),
        in_specs=[
            own(species), own(1), own(1),
            whole((ROWS, half)), whole((ROWS, half)), whole((2 * ROWS, n_cells)), whole((1, n_cells)),
        ],
        out_specs=(pl.BlockSpec((species, width), lambda i: (0, i)), whole((species, n_cells))),
        out_shape=(
            jax.ShapeDtypeStruct((species, count + slot_count), F32),
            jax.ShapeDtypeStruct((species, n_cells), F32),
        ),
        scratch_shapes=[pltpu.VMEM((ROWS + 16, 2 * n_cells), BF16)],
        compiler_params=pltpu.CompilerParams(vmem_limit_bytes=32 * 2**20),
        name="mix",
    )(reacted, cell_line, slot_line, below, above, sums, line(mixing_rate))
    return mixed, means


MCAP = 512


def solution(mesh):
    each, all_of = P("dev"), P()
    return jax.shard_map(
        functools.partial(body, slot_count=2 * MCAP),
        mesh=mesh,
        in_specs=(P(None, "dev"), each, each, each, each, each, all_of, all_of, all_of, all_of, each),
        out_specs=(P(None, "dev"), P(None, "dev")),
        check_vma=False,
    )
```

```python
import functools
import math
import jax
import jax.numpy as jnp
from jax import lax
from jax.experimental import pallas as pl
from jax.experimental.pallas import tpu as pltpu
from jax.sharding import PartitionSpec as P

NEWTON = 3
CHEM_STEP = 0.5
MIX_RATE = 0.5
LANES = 128
SUB = 512
SUBS = 2
NCOL = SUB * SUBS
CHUNK = 256
LAG = 2
ROWS = 192
UNROLL = 8
LOADS = 4
SMALL = 9
EARLY = 2
F32, BF16, I32 = jnp.float32, jnp.bfloat16, jnp.int32


def nt(a, b):
    return lax.dot_general(a, b, (((1,), (1,)), ((), ())), preferred_element_type=F32)


def nn(a, b):
    return jnp.dot(a, b, preferred_element_type=F32)


def iota(shape, dim):
    return lax.broadcasted_iota(I32, shape, dim)


def halves(x):
    hi = x.astype(BF16)
    return hi, (x - hi.astype(F32)).astype(BF16)


def hot(row, size):
    return (iota((size, row.shape[1]), 0) == row).astype(F32).astype(BF16)


def small_hot(row, size):
    which = iota((size, row.shape[1]), 0).astype(F32).astype(BF16)
    return jnp.where(which == row.astype(F32).astype(BF16), BF16(1), BF16(0))


def take(x, index):
    return jnp.take_along_axis(x, index, axis=1, mode="promise_in_bounds")


def tile_at(t, count=1):
    return pl.ds(pl.multiple_of(t * LANES, LANES), count * LANES)


def ranks(mask):
    tiles = mask.shape[0]
    upper_tri = (iota((LANES, LANES), 0) < iota((LANES, LANES), 1)).astype(F32).astype(BF16)
    lower_tri = (iota((tiles, tiles), 1) < iota((tiles, tiles), 0)).astype(F32).astype(BF16)
    half = mask.astype(BF16)
    before = jnp.sum(nn(lower_tri, half), axis=1, keepdims=True)
    return (nn(half, upper_tri) + before).astype(I32), before


def total_of(x):
    return jnp.sum(jnp.sum(x, axis=1, keepdims=True), axis=0, keepdims=True)


def react_kernel(
    states, *refs,
):
    small, refs = refs[:SMALL], refs[SMALL:]
    lower, upper, base_v, solved, *refs = refs
    held, refs = refs[:SMALL], refs[SMALL:]
    slots, rlist, mass, bins, cells, scale_row, rate_wt, stoich, jac3 = held
    (base_s, st, rank, tail, index, low_rank, jac, rate_w, stoich_w, scale, packed, stack, sem, load_sems, small_sems) = refs
    species, count = states.shape
    tiles = count // LANES
    half = lower.shape[1]
    moved_tiles = 2 * half // LANES
    most = rlist.shape[1]
    groups = ROWS // 8
    part = count // LOADS
    loads = [
        pltpu.make_async_copy(
            states.at[:, pl.ds(i * part, part)], st.at[:, pl.ds(i * part, part)], load_sems.at[i]
        )
        for i in range(LOADS)
    ]
    fetches = [pltpu.make_async_copy(small[i], held[i], small_sems.at[i]) for i in range(SMALL)]
    for copy in fetches[:EARLY] + loads + fetches[EARLY:]:
        copy.start()
    for copy in fetches[:EARLY]:
        copy.wait()

    r = rlist[...]
    listed = nt(hot(r >> 7, tiles), hot(r & 127, LANES))
    total = total_of(listed)
    moving = (slots[...] >= 0).astype(F32)
    total_move = total_of(moving)
    place, before = ranks(listed)
    place_move, before_move = ranks(moving)
    rank[...] = jnp.where(listed > 0, place, -1)
    lane = iota((tiles, LANES), 1)
    row = iota((tiles, LANES), 0)
    table = jnp.where(lane == 0, before, jnp.where(lane == 1, total, jnp.where(lane == 2, total_move, before_move)))
    for q in range(moved_tiles + 1):
        first = jnp.where((moving > 0) & (place_move == q * LANES), place.astype(F32) - total, 0.0)
        table = jnp.where((lane == 4) & (row == q), total_of(first) + total, table)
    base_v[...] = table.astype(I32)
    bases = pltpu.make_async_copy(base_v, base_s, sem)
    bases.start()
    low_rank[0] = jnp.where(listed > 0, place & 127, -1)
    low_rank[1] = jnp.where(moving > 0, place_move & 127, -1)

    for copy in fetches[EARLY:]:
        copy.wait()
    scale[...] = jnp.transpose(jnp.broadcast_to(scale_row[...], (LANES, scale_row.shape[1])))
    rate_w[...] = jnp.zeros_like(rate_w)
    rate_w[:, 0:species] = jnp.transpose(rate_wt[...].astype(F32)).astype(BF16)
    stoich_w[...] = jnp.zeros_like(stoich_w)
    stoich_w[0:species, :] = stoich[...]
    jac[...] = jnp.zeros_like(jac)
    for b in range(jac3.shape[1]):
        jac[0:species, b * ROWS : b * ROWS + species] = jac3[:, b, :]

    lanes8 = iota((8, LANES), 1).astype(F32).astype(BF16)

    def inverses(k, c):
        for u in range(UNROLL):
            t = k * UNROLL + u
            onehots = jnp.concatenate([small_hot(low_rank[s, pl.ds(t, 1), :], LANES) for s in range(2)], axis=0)
            at = pl.ds(pl.multiple_of(t * 8, 8), 8)
            index[at, :] = nt(lanes8, onehots).astype(I32)
        return c

    lax.fori_loop(0, tiles // UNROLL, inverses, 0)
    bases.wait()
    for load in loads:
        load.wait()
    rest = species - (groups - 1) * 8
    for t in range(tiles):
        at = slice(t * LANES, (t + 1) * LANES)
        rows = [mass[t : t + 1, :], (cells[t : t + 1, :] + 256 * bins[t : t + 1, :]).astype(F32),
                slots[t : t + 1, :].astype(F32), rank[t : t + 1, :].astype(F32)]
        per = tiles // 8
        solved[ROWS + t // per : ROWS + t // per + 1, t % per * LANES : (t % per + 1) * LANES] = rows[3]
        tail[0:rest, at] = st[(groups - 1) * 8 : species, at]
        for i, value in enumerate(rows):
            tail[rest + i : rest + i + 1, at] = value

    lane8 = iota((8, LANES), 1)

    def source(g, t):
        if g == groups - 1:
            return tail[:, tile_at(t)]
        return st[8 * g : 8 * g + 8, tile_at(t)]

    def compact(out, column, which, total_at):
        def some(k, carry):
            for u in range(UNROLL):
                t = k * UNROLL + u
                first = base_s[t, column]
                after = jnp.where(t == tiles - 1, base_s[0, total_at], base_s[jnp.minimum(t + 1, tiles - 1), column])
                wraps = (after >> 7) != (first >> 7)
                inside = lane8 >= (first & 127)
                picks = index[pl.ds(pl.multiple_of(t * 8, 8), 8), which * LANES : (which + 1) * LANES]
                at = tile_at(first >> 7)
                fresh = []
                for g in range(groups):
                    got = take(source(g, t), picks)
                    new = jnp.where(inside, got, carry[g])
                    out[8 * g : 8 * g + 8, at] = new
                    fresh.append(jnp.where(wraps, got, new))
                carry = tuple(fresh)
            return carry

        carry = lax.fori_loop(
            0, tiles // UNROLL, some, tuple(jnp.zeros((8, LANES), F32) for _ in range(groups))
        )
        at = tile_at(base_s[0, total_at] >> 7)
        for g in range(groups):
            out[8 * g : 8 * g + 8, at] = carry[g]

    compact(solved, 0, 0, 1)
    compact(packed, 3, 1, 2)

    reactions = rate_w.shape[0]
    chunks = [(lo, min(CHUNK, reactions - lo)) for lo in range(0, reactions, CHUNK)]

    def solve(k, c):
        subs = []
        for s in range(SUBS):
            at = pl.ds(pl.multiple_of((k * SUBS + s) * SUB, SUB), SUB)
            level = (solved[species + 1 : species + 2, at].astype(I32) >> 8).astype(F32)
            subs.append({"at": at, "start": solved[0:ROWS, at], "level": level, "d": None})
        waiting = []

        def finish():
            sub, i, u = waiting.pop(0)
            lo, size = chunks[i]
            soft = jnp.maximum(u, jnp.log(1.0 + jnp.exp(jnp.minimum(u, 87.0))))
            rate = (soft * scale[lo : lo + size, 0:1]).astype(BF16)
            term = nn(stoich_w[:, lo : lo + size], rate)
            sub["source"] = term if i == 0 else sub["source"] + term
            if i == len(chunks) - 1:
                d = sub["d"]
                residual = -CHEM_STEP * sub["source"]
                residual = (residual if d is None else d + residual).astype(BF16)
                masked = jnp.concatenate(
                    [jnp.where(sub["level"] == b, residual, BF16(0)) for b in range(jac3.shape[1])], axis=0
                )
                update = nn(jac[...], masked)
                sub["d"] = -update if d is None else d - update

        for sweep in range(NEWTON):
            for sub in subs:
                x = None
                for i, (lo, size) in enumerate(chunks):
                    if x is None:
                        x = (sub["start"] if sub["d"] is None else sub["start"] + sub["d"]).astype(BF16)
                    waiting.append((sub, i, nn(rate_w[lo : lo + size, :], x)))
                    if len(waiting) > LAG:
                        finish()
        while waiting:
            finish()
        for sub in subs:
            solved[0:ROWS, sub["at"]] = sub["start"] + sub["d"]
        return c

    lax.fori_loop(0, (base_s[0, 1] + NCOL - 1) // NCOL, solve, 0)

    spans = []
    for q in range(moved_tiles):
        low, high = base_s[q, 4], base_s[q + 1, 4]
        spans.append((low >> 7, ((high - 1) >> 7) - (low >> 7) + 1))
    longest = functools.reduce(jnp.maximum, [s[1] for s in spans])
    final = most // LANES - 1

    def expand(s, c):
        for q in range(moved_tiles):
            here = slice(q * LANES, (q + 1) * LANES)
            t = jnp.minimum(spans[q][0] + s, final)
            wanted = packed[ROWS - 1 : ROWS, here].astype(I32)
            wanted = jnp.broadcast_to(jnp.where(lane8[0:1] + q * LANES < base_s[0, 2], wanted, -1), (8, LANES))
            mine = (wanted >> 7) == t
            picks = wanted & 127
            for g in range(groups):
                rows = slice(8 * g, 8 * g + 8)
                keep = mine if g < groups - 1 else mine & (iota((8, LANES), 0) < rest)
                packed[rows, here] = jnp.where(keep, take(solved[rows, tile_at(t)], picks), packed[rows, here])
        return c

    lax.fori_loop(0, longest, expand, 0)

    mine = packed[:, 0 : 2 * half]
    filled = iota((1, 2 * half), 1) < base_s[0, 2]
    mine = jnp.where(filled, mine, 0.0)
    hi, lo = halves(mine)
    stack[0:ROWS, :] = hi
    stack[ROWS:, :] = lo
    slot = jnp.where(filled, mine[species + 2 : species + 3].astype(I32), -1)
    for out, first in ((lower, 0), (upper, half)):
        moved = nt(stack[...], hot_rows(slot - first, half))
        out[...] = moved[0:ROWS] + moved[ROWS:]


def hot_rows(row, size):
    return (iota((size, row.shape[1]), 0) == row).astype(F32).astype(BF16)


def cell_sums(x, w, cell, n_cells):
    hi, lo = halves(x * w)
    onehot = small_hot(cell, n_cells)
    return nt(jnp.concatenate([hi, lo], axis=0), onehot)


def with_ones(x):
    width = x.shape[1]
    return jnp.concatenate([x, jnp.ones((1, width), F32), jnp.zeros((ROWS - x.shape[0] - 1, width), F32)], axis=0)


def sums_kernel(base, states, solved, mass, cells, slots, reacted, sums):
    species, width = states.shape
    groups = ROWS // 8
    step = pl.program_id(0)
    lane8 = iota((8, LANES), 1)

    for b in range(width // LANES):
        here = slice(b * LANES, (b + 1) * LANES)
        first = base[step * (width // LANES) + b, 0]
        t = first >> 7
        inside = lane8 >= (first & 127)
        wanted = jnp.where(iota((8, LANES), 0) == step, solved[ROWS : ROWS + 8, here], 0.0)
        wanted = jnp.broadcast_to(jnp.sum(wanted, axis=0, keepdims=True), (8, LANES)).astype(I32)
        picks = wanted & 127
        mine = wanted >= 0
        for g in range(groups):
            n = min(8, species - 8 * g)
            rows = slice(8 * g, 8 * g + n)
            pair = jnp.where(inside[:n], solved[rows, tile_at(t)], solved[rows, tile_at(t + 1)])
            reacted[rows, here] = jnp.where(mine[:n], take(pair, picks[:n]), states[rows, here])
    w = jnp.where(slots[...] < 0, mass[...], 0.0)
    term = cell_sums(with_ones(reacted[...]), w, cells[...], sums.shape[1])

    @pl.when(step == 0)
    def _():
        sums[...] = term

    @pl.when(step > 0)
    def _():
        sums[...] += term


def arrival(ref, species):
    w = ref[species : species + 1, :]
    cell = ref[species + 1 : species + 2, :].astype(I32) & 255
    return ref[0:species, :], w, jnp.where(w > 0, cell, -1)


def mix_kernel(reacted, cells, slots, below, above, sums, mixing, mixed, means, table):
    species = reacted.shape[0]
    n_cells = sums.shape[1]
    step = pl.program_id(0)
    last = pl.num_programs(0) - 1

    @pl.when(step == 0)
    def _():
        acc = sums[...]
        for ref in (below, above):
            x, w, cell = arrival(ref, species)
            acc = acc + cell_sums(with_ones(x), w, cell, n_cells)
        acc = acc[0:ROWS] + acc[ROWS:]
        mean = acc[0:species] / acc[species : species + 1]
        means[...] = mean
        keep = jnp.exp(-MIX_RATE * mixing[...])
        table[...] = jnp.zeros_like(table)
        hi, lo = halves(mean * (1.0 - keep))
        table[0:species, 0:n_cells] = hi
        table[0:species, n_cells:] = lo
        hi, lo = halves(jnp.broadcast_to(keep, (16, n_cells)))
        table[ROWS:, 0:n_cells] = hi
        table[ROWS:, n_cells:] = lo

    def blend(x, cell):
        onehot = small_hot(cell, n_cells)
        pulled = nn(table[...], jnp.concatenate([onehot, onehot], axis=0))
        return x * pulled[ROWS : ROWS + 1] + pulled[:species]

    @pl.when(step < last)
    def _():
        mixed[...] = blend(reacted[...], jnp.where(slots[...] < 0, cells[...], -1))

    @pl.when(step == last)
    def _():
        half = below.shape[1]
        for ref, at in ((below, slice(0, half)), (above, slice(half, 2 * half))):
            x, _, cell = arrival(ref, species)
            mixed[:, at] = blend(x, cell)


def body(
    states, particle_mass, bin_index, cell_index, move_slot, react_list,
    rate_weights, stoichiometry, rate_scale, jacobian_inverse, mixing_rate, slot_count,
):
    species, count = states.shape
    n_cells = mixing_rate.shape[0]
    listed = react_list.shape[0]
    reactions = rate_scale.shape[0]
    n_bins = jacobian_inverse.shape[0]
    tiles = count // LANES
    wide = listed + 2 * LANES
    half = slot_count // 2
    square = lambda a: a.reshape(tiles, LANES)
    line = lambda a: a.reshape(1, -1)
    small = [
        square(move_slot), line(react_list), square(particle_mass), square(bin_index), square(cell_index),
        line(rate_scale), rate_weights.T, stoichiometry, jnp.transpose(jacobian_inverse, (1, 0, 2)),
    ]
    lower, upper, base, solved = pl.pallas_call(
        react_kernel,
        in_specs=[pl.BlockSpec(memory_space=pltpu.HBM)] * (1 + SMALL),
        out_shape=(
            jax.ShapeDtypeStruct((ROWS, half), F32),
            jax.ShapeDtypeStruct((ROWS, half), F32),
            jax.ShapeDtypeStruct((tiles, LANES), I32),
            jax.ShapeDtypeStruct((ROWS + 8, wide), F32),
        ),
        scratch_shapes=[pltpu.VMEM(a.shape, a.dtype) for a in small] + [
            pltpu.SMEM((tiles, LANES), I32),
            pltpu.VMEM((species, count), F32),
            pltpu.VMEM((tiles, LANES), I32),
            pltpu.VMEM((8, count), F32),
            pltpu.VMEM((tiles * 8, 2 * LANES), I32),
            pltpu.VMEM((2, tiles, LANES), I32),
            pltpu.VMEM((ROWS, n_bins * ROWS), BF16),
            pltpu.VMEM((reactions, ROWS), BF16),
            pltpu.VMEM((ROWS, reactions), BF16),
            pltpu.VMEM((reactions, LANES), F32),
            pltpu.VMEM((ROWS, slot_count + 2 * LANES), F32),
            pltpu.VMEM((2 * ROWS, slot_count), BF16),
            pltpu.SemaphoreType.DMA,
            pltpu.SemaphoreType.DMA((LOADS,)),
            pltpu.SemaphoreType.DMA((SMALL,)),
        ],
        compiler_params=pltpu.CompilerParams(vmem_limit_bytes=54 * 2**20),
        name="react",
    )(states, *small)
    devices = lax.axis_size("dev")
    below = lax.ppermute(upper, "dev", [(i, i + 1) for i in range(devices - 1)])
    above = lax.ppermute(lower, "dev", [(i + 1, i) for i in range(devices - 1)])
    width = slot_count
    steps = count // width
    own = lambda rows: pl.BlockSpec((rows, width), lambda i: (0, jnp.minimum(i, steps - 1)))
    whole = lambda shape: pl.BlockSpec(shape, lambda i: (0, 0))
    masses, cell_line, slot_line = line(particle_mass), line(cell_index), line(move_slot)
    reacted, sums = pl.pallas_call(
        sums_kernel,
        grid=(steps,),
        in_specs=[
            pl.BlockSpec(memory_space=pltpu.SMEM), own(species), whole((ROWS + 8, wide)), own(1), own(1), own(1),
        ],
        out_specs=(own(species), whole((2 * ROWS, n_cells))),
        out_shape=(jax.ShapeDtypeStruct((species, count), F32), jax.ShapeDtypeStruct((2 * ROWS, n_cells), F32)),
        compiler_params=pltpu.CompilerParams(vmem_limit_bytes=32 * 2**20),
        cost_estimate=pl.CostEstimate(
            flops=4 * ROWS * count * n_cells, bytes_accessed=8 * species * count, transcendentals=0
        ),
        name="sums",
    )(base, states, solved, masses, cell_line, slot_line)
    mixed, means = pl.pallas_call(
        mix_kernel,
        grid=(steps + 1,),
        in_specs=[
            own(species), own(1), own(1),
            whole((ROWS, half)), whole((ROWS, half)), whole((2 * ROWS, n_cells)), whole((1, n_cells)),
        ],
        out_specs=(pl.BlockSpec((species, width), lambda i: (0, i)), whole((species, n_cells))),
        out_shape=(
            jax.ShapeDtypeStruct((species, count + slot_count), F32),
            jax.ShapeDtypeStruct((species, n_cells), F32),
        ),
        scratch_shapes=[pltpu.VMEM((ROWS + 16, 2 * n_cells), BF16)],
        compiler_params=pltpu.CompilerParams(vmem_limit_bytes=32 * 2**20),
        name="mix",
    )(reacted, cell_line, slot_line, below, above, sums, line(mixing_rate))
    return mixed, means


MCAP = 512


def solution(mesh):
    each, all_of = P("dev"), P()
    return jax.shard_map(
        functools.partial(body, slot_count=2 * MCAP),
        mesh=mesh,
        in_specs=(P(None, "dev"), each, each, each, each, each, all_of, all_of, all_of, all_of, each),
        out_specs=(P(None, "dev"), P(None, "dev")),
        check_vma=False,
    )
```

```python
import functools
import math
import jax
import jax.numpy as jnp
from jax import lax
from jax.experimental import pallas as pl
from jax.experimental.pallas import tpu as pltpu
from jax.sharding import PartitionSpec as P

NEWTON = 3
CHEM_STEP = 0.5
MIX_RATE = 0.5
LANES = 128
SUB = 512
SUBS = 2
NCOL = SUB * SUBS
CHUNK = 256
LAG = 2
ROWS = 192
UNROLL = 8
LOADS = 4
SMALL = 9
EARLY = 2
MIX_PARTS = 16
F32, BF16, I32 = jnp.float32, jnp.bfloat16, jnp.int32


def nt(a, b):
    return lax.dot_general(a, b, (((1,), (1,)), ((), ())), preferred_element_type=F32)


def nn(a, b):
    return jnp.dot(a, b, preferred_element_type=F32)


def iota(shape, dim):
    return lax.broadcasted_iota(I32, shape, dim)


def halves(x):
    hi = x.astype(BF16)
    return hi, (x - hi.astype(F32)).astype(BF16)


def hot(row, size):
    return (iota((size, row.shape[1]), 0) == row).astype(F32).astype(BF16)


def small_hot(row, size):
    which = iota((size, row.shape[1]), 0).astype(F32).astype(BF16)
    return jnp.where(which == row.astype(F32).astype(BF16), BF16(1), BF16(0))


def take(x, index):
    return jnp.take_along_axis(x, index, axis=1, mode="promise_in_bounds")


def tile_at(t, count=1):
    return pl.ds(pl.multiple_of(t * LANES, LANES), count * LANES)


def ranks(mask):
    tiles = mask.shape[0]
    upper_tri = (iota((LANES, LANES), 0) < iota((LANES, LANES), 1)).astype(F32).astype(BF16)
    lower_tri = (iota((tiles, tiles), 1) < iota((tiles, tiles), 0)).astype(F32).astype(BF16)
    half = mask.astype(BF16)
    before = jnp.sum(nn(lower_tri, half), axis=1, keepdims=True)
    return (nn(half, upper_tri) + before).astype(I32), before


def total_of(x):
    return jnp.sum(jnp.sum(x, axis=1, keepdims=True), axis=0, keepdims=True)


def react_kernel(
    states, *refs,
):
    small, refs = refs[:SMALL], refs[SMALL:]
    lower, upper, base_v, solved, *refs = refs
    held, refs = refs[:SMALL], refs[SMALL:]
    slots, rlist, mass, bins, cells, scale_row, rate_wt, stoich, jac3 = held
    (base_s, st, rank, tail, index, low_rank, jac, rate_w, stoich_w, scale, packed, stack, sem, load_sems, small_sems) = refs
    species, count = states.shape
    tiles = count // LANES
    half = lower.shape[1]
    moved_tiles = 2 * half // LANES
    most = rlist.shape[1]
    groups = ROWS // 8
    part = count // LOADS
    loads = [
        pltpu.make_async_copy(
            states.at[:, pl.ds(i * part, part)], st.at[:, pl.ds(i * part, part)], load_sems.at[i]
        )
        for i in range(LOADS)
    ]
    fetches = [pltpu.make_async_copy(small[i], held[i], small_sems.at[i]) for i in range(SMALL)]
    for copy in fetches[:EARLY] + loads + fetches[EARLY:]:
        copy.start()
    for copy in fetches[:EARLY]:
        copy.wait()

    r = rlist[...]
    listed = nt(hot(r >> 7, tiles), hot(r & 127, LANES))
    total = total_of(listed)
    moving = (slots[...] >= 0).astype(F32)
    total_move = total_of(moving)
    place, before = ranks(listed)
    place_move, before_move = ranks(moving)
    rank[...] = jnp.where(listed > 0, place, -1)
    lane = iota((tiles, LANES), 1)
    row = iota((tiles, LANES), 0)
    table = jnp.where(lane == 0, before, jnp.where(lane == 1, total, jnp.where(lane == 2, total_move, before_move)))
    for q in range(moved_tiles + 1):
        first = jnp.where((moving > 0) & (place_move == q * LANES), place.astype(F32) - total, 0.0)
        table = jnp.where((lane == 4) & (row == q), total_of(first) + total, table)
    base_v[...] = table.astype(I32)
    bases = pltpu.make_async_copy(base_v, base_s, sem)
    bases.start()
    low_rank[0] = jnp.where(listed > 0, place & 127, -1)
    low_rank[1] = jnp.where(moving > 0, place_move & 127, -1)

    for copy in fetches[EARLY:]:
        copy.wait()
    scale[...] = jnp.transpose(jnp.broadcast_to(scale_row[...], (LANES, scale_row.shape[1])))
    rate_w[...] = jnp.zeros_like(rate_w)
    rate_w[:, 0:species] = jnp.transpose(rate_wt[...].astype(F32)).astype(BF16)
    stoich_w[...] = jnp.zeros_like(stoich_w)
    stoich_w[0:species, :] = stoich[...]
    jac[...] = jnp.zeros_like(jac)
    for b in range(jac3.shape[1]):
        jac[0:species, b * ROWS : b * ROWS + species] = jac3[:, b, :]

    lanes8 = iota((8, LANES), 1).astype(F32).astype(BF16)

    def inverses(k, c):
        for u in range(UNROLL):
            t = k * UNROLL + u
            onehots = jnp.concatenate([small_hot(low_rank[s, pl.ds(t, 1), :], LANES) for s in range(2)], axis=0)
            at = pl.ds(pl.multiple_of(t * 8, 8), 8)
            index[at, :] = nt(lanes8, onehots).astype(I32)
        return c

    lax.fori_loop(0, tiles // UNROLL, inverses, 0)
    bases.wait()
    for load in loads:
        load.wait()
    rest = species - (groups - 1) * 8
    for t in range(tiles):
        at = slice(t * LANES, (t + 1) * LANES)
        rows = [mass[t : t + 1, :], (cells[t : t + 1, :] + 256 * bins[t : t + 1, :]).astype(F32),
                slots[t : t + 1, :].astype(F32), rank[t : t + 1, :].astype(F32)]
        per = tiles // 8
        solved[ROWS + t // per : ROWS + t // per + 1, t % per * LANES : (t % per + 1) * LANES] = rows[3]
        tail[0:rest, at] = st[(groups - 1) * 8 : species, at]
        for i, value in enumerate(rows):
            tail[rest + i : rest + i + 1, at] = value

    lane8 = iota((8, LANES), 1)

    def source(g, t):
        if g == groups - 1:
            return tail[:, tile_at(t)]
        return st[8 * g : 8 * g + 8, tile_at(t)]

    def compact(out, column, which, total_at):
        def some(k, carry):
            for u in range(UNROLL):
                t = k * UNROLL + u
                first = base_s[t, column]
                after = jnp.where(t == tiles - 1, base_s[0, total_at], base_s[jnp.minimum(t + 1, tiles - 1), column])
                wraps = (after >> 7) != (first >> 7)
                inside = lane8 >= (first & 127)
                picks = index[pl.ds(pl.multiple_of(t * 8, 8), 8), which * LANES : (which + 1) * LANES]
                at = tile_at(first >> 7)
                fresh = []
                for g in range(groups):
                    got = take(source(g, t), picks)
                    new = jnp.where(inside, got, carry[g])
                    out[8 * g : 8 * g + 8, at] = new
                    fresh.append(jnp.where(wraps, got, new))
                carry = tuple(fresh)
            return carry

        carry = lax.fori_loop(
            0, tiles // UNROLL, some, tuple(jnp.zeros((8, LANES), F32) for _ in range(groups))
        )
        at = tile_at(base_s[0, total_at] >> 7)
        for g in range(groups):
            out[8 * g : 8 * g + 8, at] = carry[g]

    compact(solved, 0, 0, 1)
    compact(packed, 3, 1, 2)

    reactions = rate_w.shape[0]
    chunks = [(lo, min(CHUNK, reactions - lo)) for lo in range(0, reactions, CHUNK)]

    def solve(k, c):
        subs = []
        for s in range(SUBS):
            at = pl.ds(pl.multiple_of((k * SUBS + s) * SUB, SUB), SUB)
            level = (solved[species + 1 : species + 2, at].astype(I32) >> 8).astype(F32)
            subs.append({"at": at, "start": solved[0:ROWS, at], "level": level, "d": None})
        waiting = []

        def finish():
            sub, i, u = waiting.pop(0)
            lo, size = chunks[i]
            soft = jnp.maximum(u, jnp.log(1.0 + jnp.exp(jnp.minimum(u, 87.0))))
            rate = (soft * scale[lo : lo + size, 0:1]).astype(BF16)
            term = nn(stoich_w[:, lo : lo + size], rate)
            sub["source"] = term if i == 0 else sub["source"] + term
            if i == len(chunks) - 1:
                d = sub["d"]
                residual = -CHEM_STEP * sub["source"]
                residual = (residual if d is None else d + residual).astype(BF16)
                masked = jnp.concatenate(
                    [jnp.where(sub["level"] == b, residual, BF16(0)) for b in range(jac3.shape[1])], axis=0
                )
                update = nn(jac[...], masked)
                sub["d"] = -update if d is None else d - update

        for sweep in range(NEWTON):
            for sub in subs:
                x = None
                for i, (lo, size) in enumerate(chunks):
                    if x is None:
                        x = (sub["start"] if sub["d"] is None else sub["start"] + sub["d"]).astype(BF16)
                    waiting.append((sub, i, nn(rate_w[lo : lo + size, :], x)))
                    if len(waiting) > LAG:
                        finish()
        while waiting:
            finish()
        for sub in subs:
            solved[0:ROWS, sub["at"]] = sub["start"] + sub["d"]
        return c

    lax.fori_loop(0, (base_s[0, 1] + NCOL - 1) // NCOL, solve, 0)

    spans = []
    for q in range(moved_tiles):
        low, high = base_s[q, 4], base_s[q + 1, 4]
        spans.append((low >> 7, ((high - 1) >> 7) - (low >> 7) + 1))
    longest = functools.reduce(jnp.maximum, [s[1] for s in spans])
    final = most // LANES - 1

    def expand(s, c):
        for q in range(moved_tiles):
            here = slice(q * LANES, (q + 1) * LANES)
            t = jnp.minimum(spans[q][0] + s, final)
            wanted = packed[ROWS - 1 : ROWS, here].astype(I32)
            wanted = jnp.broadcast_to(jnp.where(lane8[0:1] + q * LANES < base_s[0, 2], wanted, -1), (8, LANES))
            mine = (wanted >> 7) == t
            picks = wanted & 127
            for g in range(groups):
                rows = slice(8 * g, 8 * g + 8)
                keep = mine if g < groups - 1 else mine & (iota((8, LANES), 0) < rest)
                packed[rows, here] = jnp.where(keep, take(solved[rows, tile_at(t)], picks), packed[rows, here])
        return c

    lax.fori_loop(0, longest, expand, 0)

    mine = packed[:, 0 : 2 * half]
    filled = iota((1, 2 * half), 1) < base_s[0, 2]
    mine = jnp.where(filled, mine, 0.0)
    hi, lo = halves(mine)
    stack[0:ROWS, :] = hi
    stack[ROWS:, :] = lo
    slot = jnp.where(filled, mine[species + 2 : species + 3].astype(I32), -1)
    for out, first in ((lower, 0), (upper, half)):
        moved = nt(stack[...], hot_rows(slot - first, half))
        out[...] = moved[0:ROWS] + moved[ROWS:]


def hot_rows(row, size):
    return (iota((size, row.shape[1]), 0) == row).astype(F32).astype(BF16)


def cell_sums(x, w, cell, n_cells):
    hi, lo = halves(x * w)
    onehot = small_hot(cell, n_cells)
    return nt(jnp.concatenate([hi, lo], axis=0), onehot)


def with_ones(x):
    width = x.shape[1]
    return jnp.concatenate([x, jnp.ones((1, width), F32), jnp.zeros((ROWS - x.shape[0] - 1, width), F32)], axis=0)


def sums_kernel(base, states, solved, mass, cells, slots, reacted, sums):
    species, count = states.shape
    groups = ROWS // 8
    lane8 = iota((8, LANES), 1)
    per = count // LANES // 8

    def place(step):
        for b in range(per):
            here = tile_at(step * per + b)
            first = base[step * per + b, 0]
            t = first >> 7
            inside = lane8 >= (first & 127)
            wanted = jnp.where(iota((8, LANES), 0) == step, solved[ROWS : ROWS + 8, b * LANES : (b + 1) * LANES], 0.0)
            wanted = jnp.broadcast_to(jnp.sum(wanted, axis=0, keepdims=True), (8, LANES)).astype(I32)
            picks = wanted & 127
            mine = wanted >= 0
            for g in range(groups):
                n = min(8, species - 8 * g)
                rows = slice(8 * g, 8 * g + n)
                pair = jnp.where(inside[:n], solved[rows, tile_at(t)], solved[rows, tile_at(t + 1)])
                reacted[rows, here] = jnp.where(mine[:n], take(pair, picks[:n]), states[rows, here])

    def add(step):
        at = tile_at(step * per, per)
        w = jnp.where(slots[:, at] < 0, mass[:, at], 0.0)
        sums[...] += cell_sums(with_ones(reacted[:, at]), w, cells[:, at], sums.shape[1])

    def some(step, c):
        add(step - 1)
        place(step)
        return c

    sums[...] = jnp.zeros_like(sums)
    place(0)
    lax.fori_loop(1, 8, some, 0)
    add(7)


def arrivals(below, above):
    both = jnp.concatenate([below[...], above[...]], axis=1)
    species = both.shape[0] - 4
    w = both[species : species + 1, :]
    cell = both[species + 1 : species + 2, :].astype(I32) & 255
    return both[0:species, :], w, jnp.where(w > 0, cell, -1)


def mix_kernel(reacted, cells, slots, below, above, sums, mixing, mixed, means, table, ready, sems):
    species, count = reacted.shape
    n_cells = sums.shape[1]
    width = count // MIX_PARTS
    x, w, cell = arrivals(below, above)
    acc = sums[...] + cell_sums(with_ones(x), w, cell, n_cells)
    acc = acc[0:ROWS] + acc[ROWS:]
    mean = acc[0:species] / acc[species : species + 1]
    means[...] = mean
    keep = jnp.exp(-MIX_RATE * mixing[...])
    table[...] = jnp.zeros_like(table)
    hi, lo = halves(mean * (1.0 - keep))
    table[0:species, 0:n_cells] = hi
    table[0:species, n_cells:] = lo
    hi, lo = halves(jnp.broadcast_to(keep, (16, n_cells)))
    table[ROWS:, 0:n_cells] = hi
    table[ROWS:, n_cells:] = lo

    def blend(x, cell):
        onehot = small_hot(cell, n_cells)
        pulled = nn(table[...], jnp.concatenate([onehot, onehot], axis=0))
        return x * pulled[ROWS : ROWS + 1] + pulled[:species]

    sends = []
    for step in range(ready.shape[1] // width):
        at = slice(step * width, (step + 1) * width)
        if step < MIX_PARTS:
            x, cell = reacted[:, at], jnp.where(slots[:, at] < 0, cells[:, at], -1)
        else:
            x, _, cell = arrivals(below, above)
            here = slice((step - MIX_PARTS) * width, (step - MIX_PARTS + 1) * width)
            x, cell = x[:, here], cell[:, here]
        ready[:, at] = blend(x, cell)
        sends.append(pltpu.make_async_copy(ready.at[:, at], mixed.at[:, at], sems.at[step]))
        sends[-1].start()
    for send in sends:
        send.wait()


def body(
    states, particle_mass, bin_index, cell_index, move_slot, react_list,
    rate_weights, stoichiometry, rate_scale, jacobian_inverse, mixing_rate, slot_count,
):
    species, count = states.shape
    n_cells = mixing_rate.shape[0]
    listed = react_list.shape[0]
    reactions = rate_scale.shape[0]
    n_bins = jacobian_inverse.shape[0]
    tiles = count // LANES
    wide = listed + 2 * LANES
    half = slot_count // 2
    square = lambda a: a.reshape(tiles, LANES)
    line = lambda a: a.reshape(1, -1)
    small = [
        square(move_slot), line(react_list), square(particle_mass), square(bin_index), square(cell_index),
        line(rate_scale), rate_weights.T, stoichiometry, jnp.transpose(jacobian_inverse, (1, 0, 2)),
    ]
    lower, upper, base, solved = pl.pallas_call(
        react_kernel,
        in_specs=[pl.BlockSpec(memory_space=pltpu.HBM)] * (1 + SMALL),
        out_shape=(
            jax.ShapeDtypeStruct((ROWS, half), F32),
            jax.ShapeDtypeStruct((ROWS, half), F32),
            jax.ShapeDtypeStruct((tiles, LANES), I32),
            jax.ShapeDtypeStruct((ROWS + 8, wide), F32),
        ),
        scratch_shapes=[pltpu.VMEM(a.shape, a.dtype) for a in small] + [
            pltpu.SMEM((tiles, LANES), I32),
            pltpu.VMEM((species, count), F32),
            pltpu.VMEM((tiles, LANES), I32),
            pltpu.VMEM((8, count), F32),
            pltpu.VMEM((tiles * 8, 2 * LANES), I32),
            pltpu.VMEM((2, tiles, LANES), I32),
            pltpu.VMEM((ROWS, n_bins * ROWS), BF16),
            pltpu.VMEM((reactions, ROWS), BF16),
            pltpu.VMEM((ROWS, reactions), BF16),
            pltpu.VMEM((reactions, LANES), F32),
            pltpu.VMEM((ROWS, slot_count + 2 * LANES), F32),
            pltpu.VMEM((2 * ROWS, slot_count), BF16),
            pltpu.SemaphoreType.DMA,
            pltpu.SemaphoreType.DMA((LOADS,)),
            pltpu.SemaphoreType.DMA((SMALL,)),
        ],
        compiler_params=pltpu.CompilerParams(vmem_limit_bytes=54 * 2**20),
        name="react",
    )(states, *small)
    devices = lax.axis_size("dev")
    below = lax.ppermute(upper, "dev", [(i, i + 1) for i in range(devices - 1)])
    above = lax.ppermute(lower, "dev", [(i + 1, i) for i in range(devices - 1)])
    masses, cell_line, slot_line = line(particle_mass), line(cell_index), line(move_slot)
    vmem = pl.BlockSpec(memory_space=pltpu.VMEM)
    reacted, sums = pl.pallas_call(
        sums_kernel,
        in_specs=[pl.BlockSpec(memory_space=pltpu.SMEM)] + [vmem] * 5,
        out_specs=(vmem, vmem),
        out_shape=(jax.ShapeDtypeStruct((species, count), F32), jax.ShapeDtypeStruct((2 * ROWS, n_cells), F32)),
        compiler_params=pltpu.CompilerParams(vmem_limit_bytes=32 * 2**20),
        cost_estimate=pl.CostEstimate(
            flops=4 * ROWS * count * n_cells, bytes_accessed=8 * species * count, transcendentals=0
        ),
        name="sums",
    )(base, states, solved, masses, cell_line, slot_line)
    mixed, means = pl.pallas_call(
        mix_kernel,
        in_specs=[vmem] * 7,
        out_specs=(pl.BlockSpec(memory_space=pl.ANY), vmem),
        out_shape=(
            jax.ShapeDtypeStruct((species, count + slot_count), F32),
            jax.ShapeDtypeStruct((species, n_cells), F32),
        ),
        scratch_shapes=[
            pltpu.VMEM((ROWS + 16, 2 * n_cells), BF16),
            pltpu.VMEM((species, count + slot_count), F32),
            pltpu.SemaphoreType.DMA(((count + slot_count) * MIX_PARTS // count,)),
        ],
        compiler_params=pltpu.CompilerParams(vmem_limit_bytes=32 * 2**20),
        name="mix",
    )(reacted, cell_line, slot_line, below, above, sums, line(mixing_rate))
    return mixed, means


MCAP = 512


def solution(mesh):
    each, all_of = P("dev"), P()
    return jax.shard_map(
        functools.partial(body, slot_count=2 * MCAP),
        mesh=mesh,
        in_specs=(P(None, "dev"), each, each, each, each, each, all_of, all_of, all_of, all_of, each),
        out_specs=(P(None, "dev"), P(None, "dev")),
        check_vma=False,
    )
```

```python
import functools
import math
import jax
import jax.numpy as jnp
from jax import lax
from jax.experimental import pallas as pl
from jax.experimental.pallas import tpu as pltpu
from jax.sharding import PartitionSpec as P

NEWTON = 3
CHEM_STEP = 0.5
MIX_RATE = 0.5
LANES = 128
SUB = 512
SUBS = 2
NCOL = SUB * SUBS
CHUNK = 256
LAG = 2
ROWS = 192
UNROLL = 8
LOADS = 4
SMALL = 9
EARLY = 2
MIX_PARTS = 16
F32, BF16, I32 = jnp.float32, jnp.bfloat16, jnp.int32


def nt(a, b):
    return lax.dot_general(a, b, (((1,), (1,)), ((), ())), preferred_element_type=F32)


def nn(a, b):
    return jnp.dot(a, b, preferred_element_type=F32)


def iota(shape, dim):
    return lax.broadcasted_iota(I32, shape, dim)


def halves(x):
    hi = x.astype(BF16)
    return hi, (x - hi.astype(F32)).astype(BF16)


def hot(row, size):
    return (iota((size, row.shape[1]), 0) == row).astype(F32).astype(BF16)


def small_hot(row, size):
    which = iota((size, row.shape[1]), 0).astype(F32).astype(BF16)
    return jnp.where(which == row.astype(F32).astype(BF16), BF16(1), BF16(0))


def take(x, index):
    return jnp.take_along_axis(x, index, axis=1, mode="promise_in_bounds")


def tile_at(t, count=1):
    return pl.ds(pl.multiple_of(t * LANES, LANES), count * LANES)


def ranks(mask):
    tiles = mask.shape[0]
    upper_tri = (iota((LANES, LANES), 0) < iota((LANES, LANES), 1)).astype(F32).astype(BF16)
    lower_tri = (iota((tiles, tiles), 1) < iota((tiles, tiles), 0)).astype(F32).astype(BF16)
    half = mask.astype(BF16)
    before = jnp.sum(nn(lower_tri, half), axis=1, keepdims=True)
    return (nn(half, upper_tri) + before).astype(I32), before


def total_of(x):
    return jnp.sum(jnp.sum(x, axis=1, keepdims=True), axis=0, keepdims=True)


def react_kernel(
    states, *refs,
):
    small, refs = refs[:SMALL], refs[SMALL:]
    lower, upper, base_v, solved, st, *refs = refs
    held, refs = refs[:SMALL], refs[SMALL:]
    slots, rlist, mass, bins, cells, scale_row, rate_wt, stoich, jac3 = held
    (base_s, rank, tail, index, low_rank, jac, rate_w, stoich_w, scale, packed, stack, sem, load_sems, small_sems) = refs
    species, count = states.shape
    tiles = count // LANES
    half = lower.shape[1]
    moved_tiles = 2 * half // LANES
    most = rlist.shape[1]
    groups = ROWS // 8
    part = count // LOADS
    loads = [
        pltpu.make_async_copy(
            states.at[:, pl.ds(i * part, part)], st.at[:, pl.ds(i * part, part)], load_sems.at[i]
        )
        for i in range(LOADS)
    ]
    fetches = [pltpu.make_async_copy(small[i], held[i], small_sems.at[i]) for i in range(SMALL)]
    for copy in fetches[:EARLY] + loads + fetches[EARLY:]:
        copy.start()
    for copy in fetches[:EARLY]:
        copy.wait()

    r = rlist[...]
    listed = nt(hot(r >> 7, tiles), hot(r & 127, LANES))
    total = total_of(listed)
    moving = (slots[...] >= 0).astype(F32)
    total_move = total_of(moving)
    place, before = ranks(listed)
    place_move, before_move = ranks(moving)
    rank[...] = jnp.where(listed > 0, place, -1)
    lane = iota((tiles, LANES), 1)
    row = iota((tiles, LANES), 0)
    table = jnp.where(lane == 0, before, jnp.where(lane == 1, total, jnp.where(lane == 2, total_move, before_move)))
    for q in range(moved_tiles + 1):
        first = jnp.where((moving > 0) & (place_move == q * LANES), place.astype(F32) - total, 0.0)
        table = jnp.where((lane == 4) & (row == q), total_of(first) + total, table)
    base_v[...] = table.astype(I32)
    bases = pltpu.make_async_copy(base_v, base_s, sem)
    bases.start()
    low_rank[0] = jnp.where(listed > 0, place & 127, -1)
    low_rank[1] = jnp.where(moving > 0, place_move & 127, -1)

    for copy in fetches[EARLY:]:
        copy.wait()
    scale[...] = jnp.transpose(jnp.broadcast_to(scale_row[...], (LANES, scale_row.shape[1])))
    rate_w[...] = jnp.zeros_like(rate_w)
    rate_w[:, 0:species] = jnp.transpose(rate_wt[...].astype(F32)).astype(BF16)
    stoich_w[...] = jnp.zeros_like(stoich_w)
    stoich_w[0:species, :] = stoich[...]
    jac[...] = jnp.zeros_like(jac)
    for b in range(jac3.shape[1]):
        jac[0:species, b * ROWS : b * ROWS + species] = jac3[:, b, :]

    lanes8 = iota((8, LANES), 1).astype(F32).astype(BF16)

    def inverses(k, c):
        for u in range(UNROLL):
            t = k * UNROLL + u
            onehots = jnp.concatenate([small_hot(low_rank[s, pl.ds(t, 1), :], LANES) for s in range(2)], axis=0)
            at = pl.ds(pl.multiple_of(t * 8, 8), 8)
            index[at, :] = nt(lanes8, onehots).astype(I32)
        return c

    lax.fori_loop(0, tiles // UNROLL, inverses, 0)
    bases.wait()
    for load in loads:
        load.wait()
    rest = species - (groups - 1) * 8
    for t in range(tiles):
        at = slice(t * LANES, (t + 1) * LANES)
        rows = [mass[t : t + 1, :], (cells[t : t + 1, :] + 256 * bins[t : t + 1, :]).astype(F32),
                slots[t : t + 1, :].astype(F32), rank[t : t + 1, :].astype(F32)]
        per = tiles // 8
        solved[ROWS + t // per : ROWS + t // per + 1, t % per * LANES : (t % per + 1) * LANES] = rows[3]
        tail[0:rest, at] = st[(groups - 1) * 8 : species, at]
        for i, value in enumerate(rows):
            tail[rest + i : rest + i + 1, at] = value

    lane8 = iota((8, LANES), 1)

    def source(g, t):
        if g == groups - 1:
            return tail[:, tile_at(t)]
        return st[8 * g : 8 * g + 8, tile_at(t)]

    def compact(out, column, which, total_at):
        def some(k, carry):
            for u in range(UNROLL):
                t = k * UNROLL + u
                first = base_s[t, column]
                after = jnp.where(t == tiles - 1, base_s[0, total_at], base_s[jnp.minimum(t + 1, tiles - 1), column])
                wraps = (after >> 7) != (first >> 7)
                inside = lane8 >= (first & 127)
                picks = index[pl.ds(pl.multiple_of(t * 8, 8), 8), which * LANES : (which + 1) * LANES]
                at = tile_at(first >> 7)
                fresh = []
                for g in range(groups):
                    got = take(source(g, t), picks)
                    new = jnp.where(inside, got, carry[g])
                    out[8 * g : 8 * g + 8, at] = new
                    fresh.append(jnp.where(wraps, got, new))
                carry = tuple(fresh)
            return carry

        carry = lax.fori_loop(
            0, tiles // UNROLL, some, tuple(jnp.zeros((8, LANES), F32) for _ in range(groups))
        )
        at = tile_at(base_s[0, total_at] >> 7)
        for g in range(groups):
            out[8 * g : 8 * g + 8, at] = carry[g]

    compact(solved, 0, 0, 1)
    compact(packed, 3, 1, 2)

    reactions = rate_w.shape[0]
    chunks = [(lo, min(CHUNK, reactions - lo)) for lo in range(0, reactions, CHUNK)]

    def solve(k, c):
        subs = []
        for s in range(SUBS):
            at = pl.ds(pl.multiple_of((k * SUBS + s) * SUB, SUB), SUB)
            level = (solved[species + 1 : species + 2, at].astype(I32) >> 8).astype(F32)
            subs.append({"at": at, "start": solved[0:ROWS, at], "level": level, "d": None})
        waiting = []

        def finish():
            sub, i, u = waiting.pop(0)
            lo, size = chunks[i]
            soft = jnp.maximum(u, jnp.log(1.0 + jnp.exp(jnp.minimum(u, 87.0))))
            rate = (soft * scale[lo : lo + size, 0:1]).astype(BF16)
            term = nn(stoich_w[:, lo : lo + size], rate)
            sub["source"] = term if i == 0 else sub["source"] + term
            if i == len(chunks) - 1:
                d = sub["d"]
                residual = -CHEM_STEP * sub["source"]
                residual = (residual if d is None else d + residual).astype(BF16)
                masked = jnp.concatenate(
                    [jnp.where(sub["level"] == b, residual, BF16(0)) for b in range(jac3.shape[1])], axis=0
                )
                update = nn(jac[...], masked)
                sub["d"] = -update if d is None else d - update

        for sweep in range(NEWTON):
            for sub in subs:
                x = None
                for i, (lo, size) in enumerate(chunks):
                    if x is None:
                        x = (sub["start"] if sub["d"] is None else sub["start"] + sub["d"]).astype(BF16)
                    waiting.append((sub, i, nn(rate_w[lo : lo + size, :], x)))
                    if len(waiting) > LAG:
                        finish()
        while waiting:
            finish()
        for sub in subs:
            solved[0:ROWS, sub["at"]] = sub["start"] + sub["d"]
        return c

    lax.fori_loop(0, (base_s[0, 1] + NCOL - 1) // NCOL, solve, 0)

    spans = []
    for q in range(moved_tiles):
        low, high = base_s[q, 4], base_s[q + 1, 4]
        spans.append((low >> 7, ((high - 1) >> 7) - (low >> 7) + 1))
    longest = functools.reduce(jnp.maximum, [s[1] for s in spans])
    final = most // LANES - 1

    def expand(s, c):
        for q in range(moved_tiles):
            here = slice(q * LANES, (q + 1) * LANES)
            t = jnp.minimum(spans[q][0] + s, final)
            wanted = packed[ROWS - 1 : ROWS, here].astype(I32)
            wanted = jnp.broadcast_to(jnp.where(lane8[0:1] + q * LANES < base_s[0, 2], wanted, -1), (8, LANES))
            mine = (wanted >> 7) == t
            picks = wanted & 127
            for g in range(groups):
                rows = slice(8 * g, 8 * g + 8)
                keep = mine if g < groups - 1 else mine & (iota((8, LANES), 0) < rest)
                packed[rows, here] = jnp.where(keep, take(solved[rows, tile_at(t)], picks), packed[rows, here])
        return c

    lax.fori_loop(0, longest, expand, 0)

    mine = packed[:, 0 : 2 * half]
    filled = iota((1, 2 * half), 1) < base_s[0, 2]
    mine = jnp.where(filled, mine, 0.0)
    hi, lo = halves(mine)
    stack[0:ROWS, :] = hi
    stack[ROWS:, :] = lo
    slot = jnp.where(filled, mine[species + 2 : species + 3].astype(I32), -1)
    for out, first in ((lower, 0), (upper, half)):
        moved = nt(stack[...], hot_rows(slot - first, half))
        out[...] = moved[0:ROWS] + moved[ROWS:]


def hot_rows(row, size):
    return (iota((size, row.shape[1]), 0) == row).astype(F32).astype(BF16)


def cell_sums(x, w, cell, n_cells):
    hi, lo = halves(x * w)
    onehot = small_hot(cell, n_cells)
    return nt(jnp.concatenate([hi, lo], axis=0), onehot)


def with_ones(x):
    width = x.shape[1]
    return jnp.concatenate([x, jnp.ones((1, width), F32), jnp.zeros((ROWS - x.shape[0] - 1, width), F32)], axis=0)


def sums_kernel(base, states, solved, mass, cells, slots, reacted, sums):
    species, count = states.shape
    groups = ROWS // 8
    lane8 = iota((8, LANES), 1)
    per = count // LANES // 8

    def place(step):
        for b in range(per):
            here = tile_at(step * per + b)
            first = base[step * per + b, 0]
            t = first >> 7
            inside = lane8 >= (first & 127)
            wanted = jnp.where(iota((8, LANES), 0) == step, solved[ROWS : ROWS + 8, b * LANES : (b + 1) * LANES], 0.0)
            wanted = jnp.broadcast_to(jnp.sum(wanted, axis=0, keepdims=True), (8, LANES)).astype(I32)
            picks = wanted & 127
            mine = wanted >= 0
            for g in range(groups):
                n = min(8, species - 8 * g)
                rows = slice(8 * g, 8 * g + n)
                pair = jnp.where(inside[:n], solved[rows, tile_at(t)], solved[rows, tile_at(t + 1)])
                reacted[rows, here] = jnp.where(mine[:n], take(pair, picks[:n]), states[rows, here])

    def add(step):
        at = tile_at(step * per, per)
        w = jnp.where(slots[:, at] < 0, mass[:, at], 0.0)
        sums[...] += cell_sums(with_ones(reacted[:, at]), w, cells[:, at], sums.shape[1])

    def some(step, c):
        add(step - 1)
        place(step)
        return c

    sums[...] = jnp.zeros_like(sums)
    place(0)
    lax.fori_loop(1, 8, some, 0)
    add(7)


def arrivals(below, above):
    both = jnp.concatenate([below[...], above[...]], axis=1)
    species = both.shape[0] - 4
    w = both[species : species + 1, :]
    cell = both[species + 1 : species + 2, :].astype(I32) & 255
    return both[0:species, :], w, jnp.where(w > 0, cell, -1)


def mix_kernel(reacted, cells, slots, below, above, sums, mixing, mixed, means, table, ready, sems):
    species, count = reacted.shape
    n_cells = sums.shape[1]
    width = count // MIX_PARTS
    x, w, cell = arrivals(below, above)
    acc = sums[...] + cell_sums(with_ones(x), w, cell, n_cells)
    acc = acc[0:ROWS] + acc[ROWS:]
    mean = acc[0:species] / acc[species : species + 1]
    means[...] = mean
    keep = jnp.exp(-MIX_RATE * mixing[...])
    table[...] = jnp.zeros_like(table)
    hi, lo = halves(mean * (1.0 - keep))
    table[0:species, 0:n_cells] = hi
    table[0:species, n_cells:] = lo
    hi, lo = halves(jnp.broadcast_to(keep, (16, n_cells)))
    table[ROWS:, 0:n_cells] = hi
    table[ROWS:, n_cells:] = lo

    def blend(x, cell):
        onehot = small_hot(cell, n_cells)
        pulled = nn(table[...], jnp.concatenate([onehot, onehot], axis=0))
        return x * pulled[ROWS : ROWS + 1] + pulled[:species]

    sends = []
    for step in range(ready.shape[1] // width):
        at = slice(step * width, (step + 1) * width)
        if step < MIX_PARTS:
            x, cell = reacted[:, at], jnp.where(slots[:, at] < 0, cells[:, at], -1)
        else:
            x, _, cell = arrivals(below, above)
            here = slice((step - MIX_PARTS) * width, (step - MIX_PARTS + 1) * width)
            x, cell = x[:, here], cell[:, here]
        ready[:, at] = blend(x, cell)
        sends.append(pltpu.make_async_copy(ready.at[:, at], mixed.at[:, at], sems.at[step]))
        sends[-1].start()
    for send in sends:
        send.wait()


def body(
    states, particle_mass, bin_index, cell_index, move_slot, react_list,
    rate_weights, stoichiometry, rate_scale, jacobian_inverse, mixing_rate, slot_count,
):
    species, count = states.shape
    n_cells = mixing_rate.shape[0]
    listed = react_list.shape[0]
    reactions = rate_scale.shape[0]
    n_bins = jacobian_inverse.shape[0]
    tiles = count // LANES
    wide = listed + 2 * LANES
    half = slot_count // 2
    square = lambda a: a.reshape(tiles, LANES)
    line = lambda a: a.reshape(1, -1)
    small = [
        square(move_slot), line(react_list), square(particle_mass), square(bin_index), square(cell_index),
        line(rate_scale), rate_weights.T, stoichiometry, jnp.transpose(jacobian_inverse, (1, 0, 2)),
    ]
    lower, upper, base, solved, held = pl.pallas_call(
        react_kernel,
        in_specs=[pl.BlockSpec(memory_space=pltpu.HBM)] * (1 + SMALL),
        out_shape=(
            pltpu.VMEM((ROWS, half), F32),
            pltpu.VMEM((ROWS, half), F32),
            pltpu.VMEM((tiles, LANES), I32),
            pltpu.VMEM((ROWS + 8, wide), F32),
            pltpu.VMEM((species, count), F32),
        ),
        scratch_shapes=[pltpu.VMEM(a.shape, a.dtype) for a in small] + [
            pltpu.SMEM((tiles, LANES), I32),
            pltpu.VMEM((tiles, LANES), I32),
            pltpu.VMEM((8, count), F32),
            pltpu.VMEM((tiles * 8, 2 * LANES), I32),
            pltpu.VMEM((2, tiles, LANES), I32),
            pltpu.VMEM((ROWS, n_bins * ROWS), BF16),
            pltpu.VMEM((reactions, ROWS), BF16),
            pltpu.VMEM((ROWS, reactions), BF16),
            pltpu.VMEM((reactions, LANES), F32),
            pltpu.VMEM((ROWS, slot_count + 2 * LANES), F32),
            pltpu.VMEM((2 * ROWS, slot_count), BF16),
            pltpu.SemaphoreType.DMA,
            pltpu.SemaphoreType.DMA((LOADS,)),
            pltpu.SemaphoreType.DMA((SMALL,)),
        ],
        compiler_params=pltpu.CompilerParams(vmem_limit_bytes=54 * 2**20),
        name="react",
    )(states, *small)
    devices = lax.axis_size("dev")
    below = lax.ppermute(upper, "dev", [(i, i + 1) for i in range(devices - 1)])
    above = lax.ppermute(lower, "dev", [(i + 1, i) for i in range(devices - 1)])
    masses, cell_line, slot_line = line(particle_mass), line(cell_index), line(move_slot)
    vmem = pl.BlockSpec(memory_space=pltpu.VMEM)
    reacted, sums = pl.pallas_call(
        sums_kernel,
        in_specs=[pl.BlockSpec(memory_space=pltpu.SMEM)] + [vmem] * 5,
        out_specs=(vmem, vmem),
        out_shape=(jax.ShapeDtypeStruct((species, count), F32), jax.ShapeDtypeStruct((2 * ROWS, n_cells), F32)),
        compiler_params=pltpu.CompilerParams(vmem_limit_bytes=32 * 2**20),
        cost_estimate=pl.CostEstimate(
            flops=4 * ROWS * count * n_cells, bytes_accessed=8 * species * count, transcendentals=0
        ),
        name="sums",
    )(base, held, solved, masses, cell_line, slot_line)
    mixed, means = pl.pallas_call(
        mix_kernel,
        in_specs=[vmem] * 7,
        out_specs=(pl.BlockSpec(memory_space=pl.ANY), vmem),
        out_shape=(
            jax.ShapeDtypeStruct((species, count + slot_count), F32),
            jax.ShapeDtypeStruct((species, n_cells), F32),
        ),
        scratch_shapes=[
            pltpu.VMEM((ROWS + 16, 2 * n_cells), BF16),
            pltpu.VMEM((species, count + slot_count), F32),
            pltpu.SemaphoreType.DMA(((count + slot_count) * MIX_PARTS // count,)),
        ],
        compiler_params=pltpu.CompilerParams(vmem_limit_bytes=32 * 2**20),
        name="mix",
    )(reacted, cell_line, slot_line, below, above, sums, line(mixing_rate))
    return mixed, means


MCAP = 512


def solution(mesh):
    each, all_of = P("dev"), P()
    return jax.shard_map(
        functools.partial(body, slot_count=2 * MCAP),
        mesh=mesh,
        in_specs=(P(None, "dev"), each, each, each, each, each, all_of, all_of, all_of, all_of, each),
        out_specs=(P(None, "dev"), P(None, "dev")),
        check_vma=False,
    )
```

```python
import functools
import math
import jax
import jax.numpy as jnp
from jax import lax
from jax.experimental import pallas as pl
from jax.experimental.pallas import tpu as pltpu
from jax.sharding import PartitionSpec as P

NEWTON = 3
CHEM_STEP = 0.5
MIX_RATE = 0.5
LANES = 128
SUB = 512
SUBS = 2
NCOL = SUB * SUBS
CHUNK = 256
LAG = 2
ROWS = 192
UNROLL = 8
LOADS = 4
SMALL = 9
EARLY = 2
MIX_PARTS = 16
F32, BF16, I32 = jnp.float32, jnp.bfloat16, jnp.int32


def nt(a, b):
    return lax.dot_general(a, b, (((1,), (1,)), ((), ())), preferred_element_type=F32)


def nn(a, b):
    return jnp.dot(a, b, preferred_element_type=F32)


def iota(shape, dim):
    return lax.broadcasted_iota(I32, shape, dim)


def halves(x):
    hi = x.astype(BF16)
    return hi, (x - hi.astype(F32)).astype(BF16)


def hot(row, size):
    return (iota((size, row.shape[1]), 0) == row).astype(F32).astype(BF16)


def small_hot(row, size):
    which = iota((size, row.shape[1]), 0).astype(F32).astype(BF16)
    return jnp.where(which == row.astype(F32).astype(BF16), BF16(1), BF16(0))


def take(x, index):
    return jnp.take_along_axis(x, index, axis=1, mode="promise_in_bounds")


def tile_at(t, count=1):
    return pl.ds(pl.multiple_of(t * LANES, LANES), count * LANES)


def ranks(mask):
    tiles = mask.shape[0]
    upper_tri = (iota((LANES, LANES), 0) < iota((LANES, LANES), 1)).astype(F32).astype(BF16)
    lower_tri = (iota((tiles, tiles), 1) < iota((tiles, tiles), 0)).astype(F32).astype(BF16)
    half = mask.astype(BF16)
    before = jnp.sum(nn(lower_tri, half), axis=1, keepdims=True)
    return (nn(half, upper_tri) + before).astype(I32), before


def total_of(x):
    return jnp.sum(jnp.sum(x, axis=0, keepdims=True), axis=1, keepdims=True)


def react_kernel(
    states, *refs,
):
    small, refs = refs[:SMALL], refs[SMALL:]
    lower, upper, base_v, solved, st, *refs = refs
    held, refs = refs[:SMALL], refs[SMALL:]
    slots, rlist, mass, bins, cells, scale_row, rate_wt, stoich, jac3 = held
    (base_s, rank, tail, partial, index, low_rank, jac, rate_w, stoich_w, scale, packed, stack, sem, load_sems, small_sems) = refs
    species, count = states.shape
    tiles = count // LANES
    half = lower.shape[1]
    moved_tiles = 2 * half // LANES
    most = rlist.shape[1]
    groups = ROWS // 8
    part = count // LOADS
    loads = [
        pltpu.make_async_copy(
            states.at[:, pl.ds(i * part, part)], st.at[:, pl.ds(i * part, part)], load_sems.at[i]
        )
        for i in range(LOADS)
    ]
    fetches = [pltpu.make_async_copy(small[i], held[i], small_sems.at[i]) for i in range(SMALL)]
    for copy in fetches[:EARLY] + loads + fetches[EARLY:]:
        copy.start()
    for copy in fetches[:EARLY]:
        copy.wait()

    r = rlist[...]
    listed = nt(hot(r >> 7, tiles), hot(r & 127, LANES))
    total = total_of(listed)
    moving = (slots[...] >= 0).astype(F32)
    total_move = total_of(moving)
    place, before = ranks(listed)
    place_move, before_move = ranks(moving)
    rank[...] = jnp.where(listed > 0, place, -1)
    lane = iota((tiles, LANES), 1)
    row = iota((tiles, LANES), 0)
    table = jnp.where(lane == 0, before, jnp.where(lane == 1, total, jnp.where(lane == 2, total_move, before_move)))
    for q in range(moved_tiles + 1):
        first = jnp.where((moving > 0) & (place_move == q * LANES), place.astype(F32) - total, 0.0)
        table = jnp.where((lane == 4) & (row == q), total_of(first) + total, table)
    base_v[...] = table.astype(I32)
    bases = pltpu.make_async_copy(base_v, base_s, sem)
    bases.start()
    low_rank[0] = jnp.where(listed > 0, place & 127, -1)
    low_rank[1] = jnp.where(moving > 0, place_move & 127, -1)

    for copy in fetches[EARLY:]:
        copy.wait()
    scale[...] = jnp.transpose(jnp.broadcast_to(scale_row[...], (LANES, scale_row.shape[1])))
    rate_w[...] = jnp.zeros_like(rate_w)
    rate_w[:, 0:species] = jnp.transpose(rate_wt[...].astype(F32)).astype(BF16)
    stoich_w[...] = jnp.zeros_like(stoich_w)
    stoich_w[0:species, :] = stoich[...]
    jac[...] = jnp.zeros_like(jac)
    for b in range(jac3.shape[1]):
        jac[0:species, b * ROWS : b * ROWS + species] = jac3[:, b, :]

    lanes8 = iota((8, LANES), 1).astype(F32).astype(BF16)

    def inverses(k, c):
        for u in range(UNROLL):
            t = k * UNROLL + u
            onehots = jnp.concatenate([small_hot(low_rank[s, pl.ds(t, 1), :], LANES) for s in range(2)], axis=0)
            at = pl.ds(pl.multiple_of(t * 8, 8), 8)
            index[at, :] = nt(lanes8, onehots).astype(I32)
        return c

    inverses(0, 0)
    bases.wait()
    for load in loads:
        load.wait()
    rest = species - (groups - 1) * 8
    for t in range(tiles):
        at = slice(t * LANES, (t + 1) * LANES)
        rows = [mass[t : t + 1, :], (cells[t : t + 1, :] + 256 * bins[t : t + 1, :]).astype(F32),
                slots[t : t + 1, :].astype(F32), rank[t : t + 1, :].astype(F32)]
        per = tiles // 8
        solved[ROWS + t // per : ROWS + t // per + 1, t % per * LANES : (t % per + 1) * LANES] = rows[3]
        tail[0:rest, at] = st[(groups - 1) * 8 : species, at]
        for i, value in enumerate(rows):
            tail[rest + i : rest + i + 1, at] = value

    lane8 = iota((8, LANES), 1)

    def source(g, t):
        if g == groups - 1:
            return tail[:, tile_at(t)]
        return st[8 * g : 8 * g + 8, tile_at(t)]

    def compact_tile(out, column, which, total_at, t, carry):
        first = base_s[t, column]
        after = jnp.where(t == tiles - 1, base_s[0, total_at], base_s[jnp.minimum(t + 1, tiles - 1), column])
        wraps = (after >> 7) != (first >> 7)
        inside = lane8 >= (first & 127)
        picks = index[pl.ds(pl.multiple_of(t * 8, 8), 8), which * LANES : (which + 1) * LANES]
        at = tile_at(first >> 7)
        fresh = []
        for g in range(groups):
            got = take(source(g, t), picks)
            new = jnp.where(inside, got, carry[g])
            out[8 * g : 8 * g + 8, at] = new
            fresh.append(jnp.where(wraps, got, new))
        return tuple(fresh)

    def compact(out, column, which, total_at, begin, carry, beside):
        def some(k, carry):
            for u in range(UNROLL):
                carry = compact_tile(out, column, which, total_at, k * UNROLL + u, carry)
            beside(k)
            return carry

        carry = lax.fori_loop(begin, tiles // UNROLL, some, carry)
        at = tile_at(base_s[0, total_at] >> 7)
        for g in range(groups):
            out[8 * g : 8 * g + 8, at] = carry[g]

    empty = tuple(jnp.zeros((8, LANES), F32) for _ in range(groups))
    following = lambda k: inverses(jnp.minimum(k + 1, tiles // UNROLL - 1), 0)
    compact(solved, 0, 0, 1, 0, empty, following)
    partial[...] = jnp.zeros_like(partial)
    load_partial = lambda: tuple(partial[8 * g : 8 * g + 8, :] for g in range(groups))
    beside_step = tiles * NCOL // most

    reactions = rate_w.shape[0]
    chunks = [(lo, min(CHUNK, reactions - lo)) for lo in range(0, reactions, CHUNK)]

    def solve(k, c):
        subs = []
        for s in range(SUBS):
            at = pl.ds(pl.multiple_of((k * SUBS + s) * SUB, SUB), SUB)
            level = (solved[species + 1 : species + 2, at].astype(I32) >> 8).astype(F32)
            subs.append({"at": at, "start": solved[0:ROWS, at], "level": level, "d": None})
        waiting = []
        finishes = NEWTON * SUBS * len(chunks)
        moved = {"carry": load_partial(), "done": 0, "finished": 0}

        def move_some():
            moved["finished"] += 1
            while moved["done"] * finishes < beside_step * moved["finished"]:
                t = k * beside_step + moved["done"]
                moved["carry"] = compact_tile(packed, 3, 1, 2, t, moved["carry"])
                moved["done"] += 1

        def finish():
            sub, i, u = waiting.pop(0)
            lo, size = chunks[i]
            soft = jnp.maximum(u, jnp.log(1.0 + jnp.exp(jnp.minimum(u, 87.0))))
            rate = (soft * scale[lo : lo + size, 0:1]).astype(BF16)
            term = nn(stoich_w[:, lo : lo + size], rate)
            sub["source"] = term if i == 0 else sub["source"] + term
            if i == len(chunks) - 1:
                d = sub["d"]
                residual = -CHEM_STEP * sub["source"]
                residual = (residual if d is None else d + residual).astype(BF16)
                masked = jnp.concatenate(
                    [jnp.where(sub["level"] == b, residual, BF16(0)) for b in range(jac3.shape[1])], axis=0
                )
                update = nn(jac[...], masked)
                sub["d"] = -update if d is None else d - update

        for sweep in range(NEWTON):
            for sub in subs:
                x = None
                for i, (lo, size) in enumerate(chunks):
                    if x is None:
                        x = (sub["start"] if sub["d"] is None else sub["start"] + sub["d"]).astype(BF16)
                    waiting.append((sub, i, nn(rate_w[lo : lo + size, :], x)))
                    if len(waiting) > LAG:
                        finish()
                        move_some()
        while waiting:
            finish()
            move_some()
        for g in range(groups):
            partial[8 * g : 8 * g + 8, :] = moved["carry"][g]
        for sub in subs:
            solved[0:ROWS, sub["at"]] = sub["start"] + sub["d"]
        return c

    steps = (base_s[0, 1] + NCOL - 1) // NCOL
    lax.fori_loop(0, steps, solve, 0)
    compact(packed, 3, 1, 2, steps * (beside_step // UNROLL), load_partial(), lambda k: None)

    spans = []
    for q in range(moved_tiles):
        low, high = base_s[q, 4], base_s[q + 1, 4]
        spans.append((low >> 7, ((high - 1) >> 7) - (low >> 7) + 1))
    longest = functools.reduce(jnp.maximum, [s[1] for s in spans])
    final = most // LANES - 1

    def expand(s, c):
        for q in range(moved_tiles):
            here = slice(q * LANES, (q + 1) * LANES)
            t = jnp.minimum(spans[q][0] + s, final)
            wanted = packed[ROWS - 1 : ROWS, here].astype(I32)
            wanted = jnp.broadcast_to(jnp.where(lane8[0:1] + q * LANES < base_s[0, 2], wanted, -1), (8, LANES))
            mine = (wanted >> 7) == t
            picks = wanted & 127
            for g in range(groups):
                rows = slice(8 * g, 8 * g + 8)
                keep = mine if g < groups - 1 else mine & (iota((8, LANES), 0) < rest)
                packed[rows, here] = jnp.where(keep, take(solved[rows, tile_at(t)], picks), packed[rows, here])
        return c

    lax.fori_loop(0, longest, expand, 0)

    mine = packed[:, 0 : 2 * half]
    filled = iota((1, 2 * half), 1) < base_s[0, 2]
    mine = jnp.where(filled, mine, 0.0)
    hi, lo = halves(mine)
    stack[0:ROWS, :] = hi
    stack[ROWS:, :] = lo
    slot = jnp.where(filled, mine[species + 2 : species + 3].astype(I32), -1)
    for out, first in ((lower, 0), (upper, half)):
        moved = nt(stack[...], hot_rows(slot - first, half))
        out[...] = moved[0:ROWS] + moved[ROWS:]


def hot_rows(row, size):
    return (iota((size, row.shape[1]), 0) == row).astype(F32).astype(BF16)


def cell_sums(x, w, cell, n_cells):
    hi, lo = halves(x * w)
    onehot = small_hot(cell, n_cells)
    return nt(jnp.concatenate([hi, lo], axis=0), onehot)


def with_ones(x):
    width = x.shape[1]
    return jnp.concatenate([x, jnp.ones((1, width), F32), jnp.zeros((ROWS - x.shape[0] - 1, width), F32)], axis=0)


def sums_kernel(base, states, solved, mass, cells, slots, reacted, sums):
    species, count = states.shape
    groups = ROWS // 8
    lane8 = iota((8, LANES), 1)
    per = count // LANES // 8

    def place(step):
        for b in range(per):
            here = tile_at(step * per + b)
            first = base[step * per + b, 0]
            t = first >> 7
            inside = lane8 >= (first & 127)
            wanted = jnp.where(iota((8, LANES), 0) == step, solved[ROWS : ROWS + 8, b * LANES : (b + 1) * LANES], 0.0)
            wanted = jnp.broadcast_to(jnp.sum(wanted, axis=0, keepdims=True), (8, LANES)).astype(I32)
            picks = wanted & 127
            mine = wanted >= 0
            for g in range(groups):
                n = min(8, species - 8 * g)
                rows = slice(8 * g, 8 * g + n)
                pair = jnp.where(inside[:n], solved[rows, tile_at(t)], solved[rows, tile_at(t + 1)])
                reacted[rows, here] = jnp.where(mine[:n], take(pair, picks[:n]), states[rows, here])

    def add(step):
        at = tile_at(step * per, per)
        w = jnp.where(slots[:, at] < 0, mass[:, at], 0.0)
        sums[...] += cell_sums(with_ones(reacted[:, at]), w, cells[:, at], sums.shape[1])

    def some(step, c):
        add(step - 1)
        place(step)
        return c

    sums[...] = jnp.zeros_like(sums)
    place(0)
    lax.fori_loop(1, 8, some, 0)
    add(7)


def arrivals(below, above):
    both = jnp.concatenate([below[...], above[...]], axis=1)
    species = both.shape[0] - 4
    w = both[species : species + 1, :]
    cell = both[species + 1 : species + 2, :].astype(I32) & 255
    return both[0:species, :], w, jnp.where(w > 0, cell, -1)


def mix_kernel(reacted, cells, slots, below, above, sums, mixing, mixed, means, table, ready, sems):
    species, count = reacted.shape
    n_cells = sums.shape[1]
    width = count // MIX_PARTS
    x, w, cell = arrivals(below, above)
    acc = sums[...] + cell_sums(with_ones(x), w, cell, n_cells)
    acc = acc[0:ROWS] + acc[ROWS:]
    mean = acc[0:species] / acc[species : species + 1]
    means[...] = mean
    keep = jnp.exp(-MIX_RATE * mixing[...])
    table[...] = jnp.zeros_like(table)
    hi, lo = halves(mean * (1.0 - keep))
    table[0:species, 0:n_cells] = hi
    table[0:species, n_cells:] = lo
    hi, lo = halves(jnp.broadcast_to(keep, (16, n_cells)))
    table[ROWS:, 0:n_cells] = hi
    table[ROWS:, n_cells:] = lo

    def blend(x, cell):
        onehot = small_hot(cell, n_cells)
        pulled = nn(table[...], jnp.concatenate([onehot, onehot], axis=0))
        return x * pulled[ROWS : ROWS + 1] + pulled[:species]

    sends = []
    for step in range(ready.shape[1] // width):
        at = slice(step * width, (step + 1) * width)
        if step < MIX_PARTS:
            x, cell = reacted[:, at], jnp.where(slots[:, at] < 0, cells[:, at], -1)
        else:
            x, _, cell = arrivals(below, above)
            here = slice((step - MIX_PARTS) * width, (step - MIX_PARTS + 1) * width)
            x, cell = x[:, here], cell[:, here]
        ready[:, at] = blend(x, cell)
        sends.append(pltpu.make_async_copy(ready.at[:, at], mixed.at[:, at], sems.at[step]))
        sends[-1].start()
    for send in sends:
        send.wait()


def body(
    states, particle_mass, bin_index, cell_index, move_slot, react_list,
    rate_weights, stoichiometry, rate_scale, jacobian_inverse, mixing_rate, slot_count,
):
    species, count = states.shape
    n_cells = mixing_rate.shape[0]
    listed = react_list.shape[0]
    reactions = rate_scale.shape[0]
    n_bins = jacobian_inverse.shape[0]
    tiles = count // LANES
    wide = listed + 2 * LANES
    half = slot_count // 2
    square = lambda a: a.reshape(tiles, LANES)
    line = lambda a: a.reshape(1, -1)
    small = [
        square(move_slot), line(react_list), square(particle_mass), square(bin_index), square(cell_index),
        line(rate_scale), rate_weights.T, stoichiometry, jnp.transpose(jacobian_inverse, (1, 0, 2)),
    ]
    lower, upper, base, solved, held = pl.pallas_call(
        react_kernel,
        in_specs=[pl.BlockSpec(memory_space=pltpu.HBM)] * (1 + SMALL),
        out_shape=(
            pltpu.VMEM((ROWS, half), F32),
            pltpu.VMEM((ROWS, half), F32),
            pltpu.VMEM((tiles, LANES), I32),
            pltpu.VMEM((ROWS + 8, wide), F32),
            pltpu.VMEM((species, count), F32),
        ),
        scratch_shapes=[pltpu.VMEM(a.shape, a.dtype) for a in small] + [
            pltpu.SMEM((tiles, LANES), I32),
            pltpu.VMEM((tiles, LANES), I32),
            pltpu.VMEM((8, count), F32),
            pltpu.VMEM((ROWS, LANES), F32),
            pltpu.VMEM((tiles * 8, 2 * LANES), I32),
            pltpu.VMEM((2, tiles, LANES), I32),
            pltpu.VMEM((ROWS, n_bins * ROWS), BF16),
            pltpu.VMEM((reactions, ROWS), BF16),
            pltpu.VMEM((ROWS, reactions), BF16),
            pltpu.VMEM((reactions, LANES), F32),
            pltpu.VMEM((ROWS, slot_count + 2 * LANES), F32),
            pltpu.VMEM((2 * ROWS, slot_count), BF16),
            pltpu.SemaphoreType.DMA,
            pltpu.SemaphoreType.DMA((LOADS,)),
            pltpu.SemaphoreType.DMA((SMALL,)),
        ],
        compiler_params=pltpu.CompilerParams(vmem_limit_bytes=54 * 2**20),
        name="react",
    )(states, *small)
    devices = lax.axis_size("dev")
    below = lax.ppermute(upper, "dev", [(i, i + 1) for i in range(devices - 1)])
    above = lax.ppermute(lower, "dev", [(i + 1, i) for i in range(devices - 1)])
    masses, cell_line, slot_line = line(particle_mass), line(cell_index), line(move_slot)
    vmem = pl.BlockSpec(memory_space=pltpu.VMEM)
    reacted, sums = pl.pallas_call(
        sums_kernel,
        in_specs=[pl.BlockSpec(memory_space=pltpu.SMEM)] + [vmem] * 5,
        out_specs=(vmem, vmem),
        out_shape=(jax.ShapeDtypeStruct((species, count), F32), jax.ShapeDtypeStruct((2 * ROWS, n_cells), F32)),
        compiler_params=pltpu.CompilerParams(vmem_limit_bytes=32 * 2**20),
        cost_estimate=pl.CostEstimate(
            flops=4 * ROWS * count * n_cells, bytes_accessed=8 * species * count, transcendentals=0
        ),
        name="sums",
    )(base, held, solved, masses, cell_line, slot_line)
    mixed, means = pl.pallas_call(
        mix_kernel,
        in_specs=[vmem] * 7,
        out_specs=(pl.BlockSpec(memory_space=pl.ANY), vmem),
        out_shape=(
            jax.ShapeDtypeStruct((species, count + slot_count), F32),
            jax.ShapeDtypeStruct((species, n_cells), F32),
        ),
        scratch_shapes=[
            pltpu.VMEM((ROWS + 16, 2 * n_cells), BF16),
            pltpu.VMEM((species, count + slot_count), F32),
            pltpu.SemaphoreType.DMA(((count + slot_count) * MIX_PARTS // count,)),
        ],
        compiler_params=pltpu.CompilerParams(vmem_limit_bytes=32 * 2**20),
        name="mix",
    )(reacted, cell_line, slot_line, below, above, sums, line(mixing_rate))
    return mixed, means


MCAP = 512


def solution(mesh):
    each, all_of = P("dev"), P()
    return jax.shard_map(
        functools.partial(body, slot_count=2 * MCAP),
        mesh=mesh,
        in_specs=(P(None, "dev"), each, each, each, each, each, all_of, all_of, all_of, all_of, each),
        out_specs=(P(None, "dev"), P(None, "dev")),
        check_vma=False,
    )
```

```python
import functools
import math
import jax
import jax.numpy as jnp
from jax import lax
from jax.experimental import pallas as pl
from jax.experimental.pallas import tpu as pltpu
from jax.sharding import PartitionSpec as P

NEWTON = 3
CHEM_STEP = 0.5
MIX_RATE = 0.5
LANES = 128
SUB = 512
SUBS = 2
NCOL = SUB * SUBS
CHUNK = 256
LAG = 2
ROWS = 192
UNROLL = 8
LOADS = 4
SMALL = 9
EARLY = 2
MIX_PARTS = 16
F32, BF16, I32 = jnp.float32, jnp.bfloat16, jnp.int32


def nt(a, b):
    return lax.dot_general(a, b, (((1,), (1,)), ((), ())), preferred_element_type=F32)


def nn(a, b):
    return jnp.dot(a, b, preferred_element_type=F32)


def iota(shape, dim):
    return lax.broadcasted_iota(I32, shape, dim)


def halves(x):
    hi = x.astype(BF16)
    return hi, (x - hi.astype(F32)).astype(BF16)


def hot(row, size):
    return (iota((size, row.shape[1]), 0) == row).astype(F32).astype(BF16)


def small_hot(row, size):
    which = iota((size, row.shape[1]), 0).astype(F32).astype(BF16)
    return jnp.where(which == row.astype(F32).astype(BF16), BF16(1), BF16(0))


def take(x, index):
    return jnp.take_along_axis(x, index, axis=1, mode="promise_in_bounds")


def tile_at(t, count=1):
    return pl.ds(pl.multiple_of(t * LANES, LANES), count * LANES)


def ranks(mask):
    tiles = mask.shape[0]
    upper_tri = (iota((LANES, LANES), 0) < iota((LANES, LANES), 1)).astype(F32).astype(BF16)
    lower_tri = (iota((tiles, tiles), 1) < iota((tiles, tiles), 0)).astype(F32).astype(BF16)
    half = mask.astype(BF16)
    before = jnp.sum(nn(lower_tri, half), axis=1, keepdims=True)
    return (nn(half, upper_tri) + before).astype(I32), before


def total_of(x):
    return jnp.sum(jnp.sum(x, axis=0, keepdims=True), axis=1, keepdims=True)


def react_kernel(
    states, *refs,
):
    small, refs = refs[:SMALL], refs[SMALL:]
    lower, upper, base_v, solved, st, *refs = refs
    held, refs = refs[:SMALL], refs[SMALL:]
    slots, rlist, mass, bins, cells, scale_row, rate_wt, stoich, jac3 = held
    (base_s, rank, tail, partial, index, low_rank, jac, rate_w, stoich_w, scale, packed, stack, sem, load_sems, small_sems) = refs
    species, count = states.shape
    tiles = count // LANES
    half = lower.shape[1]
    moved_tiles = 2 * half // LANES
    most = rlist.shape[1]
    groups = ROWS // 8
    part = count // LOADS
    loads = [
        pltpu.make_async_copy(
            states.at[:, pl.ds(i * part, part)], st.at[:, pl.ds(i * part, part)], load_sems.at[i]
        )
        for i in range(LOADS)
    ]
    fetches = [pltpu.make_async_copy(small[i], held[i], small_sems.at[i]) for i in range(SMALL)]
    for copy in fetches[:EARLY] + loads + fetches[EARLY:]:
        copy.start()
    for copy in fetches[:EARLY]:
        copy.wait()

    r = rlist[...]
    listed = nt(hot(r >> 7, tiles), hot(r & 127, LANES))
    total = total_of(listed)
    moving = (slots[...] >= 0).astype(F32)
    total_move = total_of(moving)
    place, before = ranks(listed)
    place_move, before_move = ranks(moving)
    rank[...] = jnp.where(listed > 0, place, -1)
    lane = iota((tiles, LANES), 1)
    row = iota((tiles, LANES), 0)
    table = jnp.where(lane == 0, before, jnp.where(lane == 1, total, jnp.where(lane == 2, total_move, before_move)))
    for q in range(moved_tiles + 1):
        first = jnp.where((moving > 0) & (place_move == q * LANES), place.astype(F32) - total, 0.0)
        table = jnp.where((lane == 4) & (row == q), total_of(first) + total, table)
    base_v[...] = table.astype(I32)
    bases = pltpu.make_async_copy(base_v, base_s, sem)
    bases.start()
    low_rank[0] = jnp.where(listed > 0, place & 127, -1)
    low_rank[1] = jnp.where(moving > 0, place_move & 127, -1)

    for copy in fetches[EARLY:]:
        copy.wait()
    scale[...] = jnp.transpose(jnp.broadcast_to(scale_row[...], (LANES, scale_row.shape[1])))
    rate_w[...] = jnp.zeros_like(rate_w)
    rate_w[:, 0:species] = jnp.transpose(rate_wt[...].astype(F32)).astype(BF16)
    stoich_w[...] = jnp.zeros_like(stoich_w)
    stoich_w[0:species, :] = stoich[...]
    jac[...] = jnp.zeros_like(jac)
    for b in range(jac3.shape[1]):
        jac[0:species, b * ROWS : b * ROWS + species] = jac3[:, b, :]

    lanes8 = iota((8, LANES), 1).astype(F32).astype(BF16)

    def inverses(k, c):
        for u in range(UNROLL):
            t = k * UNROLL + u
            onehots = jnp.concatenate([small_hot(low_rank[s, pl.ds(t, 1), :], LANES) for s in range(2)], axis=0)
            at = pl.ds(pl.multiple_of(t * 8, 8), 8)
            index[at, :] = nt(lanes8, onehots).astype(I32)
        return c

    inverses(0, 0)
    bases.wait()
    for load in loads:
        load.wait()
    rest = species - (groups - 1) * 8
    for t in range(tiles):
        at = slice(t * LANES, (t + 1) * LANES)
        rows = [mass[t : t + 1, :], (cells[t : t + 1, :] + 256 * bins[t : t + 1, :]).astype(F32),
                slots[t : t + 1, :].astype(F32), rank[t : t + 1, :].astype(F32)]
        per = tiles // 8
        solved[ROWS + t // per : ROWS + t // per + 1, t % per * LANES : (t % per + 1) * LANES] = rows[3]
        tail[0:rest, at] = st[(groups - 1) * 8 : species, at]
        for i, value in enumerate(rows):
            tail[rest + i : rest + i + 1, at] = value

    lane8 = iota((8, LANES), 1)

    def source(g, t):
        if g == groups - 1:
            return tail[:, tile_at(t)]
        return st[8 * g : 8 * g + 8, tile_at(t)]

    def compact_tile(out, column, which, total_at, t, carry):
        first = base_s[t, column]
        after = jnp.where(t == tiles - 1, base_s[0, total_at], base_s[jnp.minimum(t + 1, tiles - 1), column])
        wraps = (after >> 7) != (first >> 7)
        inside = lane8 >= (first & 127)
        picks = index[pl.ds(pl.multiple_of(t * 8, 8), 8), which * LANES : (which + 1) * LANES]
        at = tile_at(first >> 7)
        fresh = []
        for g in range(groups):
            got = take(source(g, t), picks)
            new = jnp.where(inside, got, carry[g])
            out[8 * g : 8 * g + 8, at] = new
            fresh.append(jnp.where(wraps, got, new))
        return tuple(fresh)

    def compact(out, column, which, total_at, begin, carry, beside):
        def some(k, carry):
            for u in range(UNROLL):
                carry = compact_tile(out, column, which, total_at, k * UNROLL + u, carry)
            beside(k)
            return carry

        carry = lax.fori_loop(begin, tiles // UNROLL, some, carry)
        at = tile_at(base_s[0, total_at] >> 7)
        for g in range(groups):
            out[8 * g : 8 * g + 8, at] = carry[g]

    empty = tuple(jnp.zeros((8, LANES), F32) for _ in range(groups))
    following = lambda k: inverses(jnp.minimum(k + 1, tiles // UNROLL - 1), 0)
    compact(solved, 0, 0, 1, 0, empty, following)
    partial[...] = jnp.zeros_like(partial)
    load_partial = lambda: tuple(partial[8 * g : 8 * g + 8, :] for g in range(groups))
    beside_step = tiles * NCOL // most

    reactions = rate_w.shape[0]
    chunks = [(lo, min(CHUNK, reactions - lo)) for lo in range(0, reactions, CHUNK)]

    def solve(k, c):
        subs = []
        for s in range(SUBS):
            at = pl.ds(pl.multiple_of((k * SUBS + s) * SUB, SUB), SUB)
            level = (solved[species + 1 : species + 2, at].astype(I32) >> 8).astype(F32)
            subs.append({"at": at, "start": solved[0:ROWS, at], "level": level, "d": None})
        waiting = []
        finishes = NEWTON * SUBS * len(chunks)
        moved = {"carry": load_partial(), "done": 0, "finished": 0}

        def move_some():
            moved["finished"] += 1
            while moved["done"] * finishes < beside_step * moved["finished"]:
                t = k * beside_step + moved["done"]
                moved["carry"] = compact_tile(packed, 3, 1, 2, t, moved["carry"])
                moved["done"] += 1

        def finish():
            sub, i, u = waiting.pop(0)
            lo, size = chunks[i]
            soft = jnp.maximum(u, jnp.log(1.0 + jnp.exp(jnp.minimum(u, 87.0))))
            rate = (soft * scale[lo : lo + size, 0:1]).astype(BF16)
            term = nn(stoich_w[:, lo : lo + size], rate)
            sub["source"] = term if i == 0 else sub["source"] + term
            if i == len(chunks) - 1:
                d = sub["d"]
                residual = -CHEM_STEP * sub["source"]
                residual = (residual if d is None else d + residual).astype(BF16)
                masked = jnp.concatenate(
                    [jnp.where(sub["level"] == b, residual, BF16(0)) for b in range(jac3.shape[1])], axis=0
                )
                update = nn(jac[...], masked)
                sub["d"] = -update if d is None else d - update

        for sweep in range(NEWTON):
            for sub in subs:
                x = None
                for i, (lo, size) in enumerate(chunks):
                    if x is None:
                        x = (sub["start"] if sub["d"] is None else sub["start"] + sub["d"]).astype(BF16)
                    waiting.append((sub, i, nn(rate_w[lo : lo + size, :], x)))
                    if len(waiting) > LAG:
                        finish()
                        move_some()
        while waiting:
            finish()
            move_some()
        for g in range(groups):
            partial[8 * g : 8 * g + 8, :] = moved["carry"][g]
        for sub in subs:
            solved[0:ROWS, sub["at"]] = sub["start"] + sub["d"]
        return c

    steps = (base_s[0, 1] + NCOL - 1) // NCOL
    lax.fori_loop(0, steps, solve, 0)
    compact(packed, 3, 1, 2, steps * (beside_step // UNROLL), load_partial(), lambda k: None)

    spans = []
    for q in range(moved_tiles):
        low, high = base_s[q, 4], base_s[q + 1, 4]
        spans.append((low >> 7, ((high - 1) >> 7) - (low >> 7) + 1))
    longest = functools.reduce(jnp.maximum, [s[1] for s in spans])
    final = most // LANES - 1

    def expand(s, c):
        for q in range(moved_tiles):
            here = slice(q * LANES, (q + 1) * LANES)
            t = jnp.minimum(spans[q][0] + s, final)
            wanted = packed[ROWS - 1 : ROWS, here].astype(I32)
            wanted = jnp.broadcast_to(jnp.where(lane8[0:1] + q * LANES < base_s[0, 2], wanted, -1), (8, LANES))
            mine = (wanted >> 7) == t
            picks = wanted & 127
            for g in range(groups):
                rows = slice(8 * g, 8 * g + 8)
                keep = mine if g < groups - 1 else mine & (iota((8, LANES), 0) < rest)
                packed[rows, here] = jnp.where(keep, take(solved[rows, tile_at(t)], picks), packed[rows, here])
        return c

    lax.fori_loop(0, longest, expand, 0)

    mine = packed[:, 0 : 2 * half]
    filled = iota((1, 2 * half), 1) < base_s[0, 2]
    mine = jnp.where(filled, mine, 0.0)
    hi, lo = halves(mine)
    stack[0:ROWS, :] = hi
    stack[ROWS:, :] = lo
    slot = jnp.where(filled, mine[species + 2 : species + 3].astype(I32), -1)
    for out, first in ((lower, 0), (upper, half)):
        moved = nt(stack[...], hot_rows(slot - first, half))
        out[...] = moved[0:ROWS] + moved[ROWS:]


def hot_rows(row, size):
    return (iota((size, row.shape[1]), 0) == row).astype(F32).astype(BF16)


def cell_sums(x, w, cell, n_cells):
    hi, lo = halves(x * w)
    onehot = small_hot(cell, n_cells)
    return nt(jnp.concatenate([hi, lo], axis=0), onehot)


def with_ones(x):
    width = x.shape[1]
    return jnp.concatenate([x, jnp.ones((1, width), F32), jnp.zeros((ROWS - x.shape[0] - 1, width), F32)], axis=0)


def exchange_kernel(
    devices, base, states, solved, mass, cells, slots, lower, upper, sums, below, above, sent, got,
):
    me = lax.axis_index("dev")
    after, before = lax.rem(me + 1, devices), lax.rem(me + devices - 1, devices)
    has_after, has_before = me < devices - 1, me > 0
    barrier = pltpu.get_barrier_semaphore()
    for there, other in ((has_after, after), (has_before, before)):
        @pl.when(there)
        def _(other=other):
            pl.semaphore_signal(barrier, inc=1, device_id=(other,), device_id_type=pl.DeviceIdType.MESH)
    inner = has_after & has_before

    @pl.when(inner)
    def _():
        pl.semaphore_wait(barrier, 2)

    @pl.when(jnp.logical_not(inner))
    def _():
        pl.semaphore_wait(barrier, 1)

    def transfer(i, src, dst, other):
        return pltpu.make_async_remote_copy(
            src_ref=src, dst_ref=dst, send_sem=sent.at[i], recv_sem=got.at[i],
            device_id=(other,), device_id_type=pl.DeviceIdType.MESH,
        )

    up, down = transfer(0, upper, below, after), transfer(1, lower, above, before)

    @pl.when(has_after)
    def _():
        up.start()

    @pl.when(has_before)
    def _():
        down.start()

    @pl.when(me == 0)
    def _():
        below[...] = jnp.zeros_like(below)

    @pl.when(me == devices - 1)
    def _():
        above[...] = jnp.zeros_like(above)

    species, count = states.shape
    per = count // LANES // 8
    width = per * LANES
    total = base[0:1, 1:2]

    def add(step, c):
        at = tile_at(step * per, per)
        rank = jnp.where(iota((8, width), 0) == step, solved[ROWS : ROWS + 8, 0:width], 0.0)
        idle = (slots[:, at] < 0) & (jnp.sum(rank, axis=0, keepdims=True) < 0)
        w = jnp.where(idle, mass[:, at], 0.0)
        sums[...] += cell_sums(with_ones(states[:, at]), w, cells[:, at], sums.shape[1])
        return c

    def add_solved(step, c):
        at = tile_at(step * per, per)
        valid = iota((1, width), 1) + step * width < total
        x = jnp.where(valid, solved[0:ROWS, at], 0.0)
        w = jnp.where(valid & (x[species + 2 : species + 3] < 0), x[species : species + 1], 0.0)
        cell = x[species + 1 : species + 2].astype(I32) & 255
        sums[...] += cell_sums(with_ones(x[0:species]), w, cell, sums.shape[1])
        return c

    sums[...] = jnp.zeros_like(sums)
    lax.fori_loop(0, 8, add, 0)
    lax.fori_loop(0, solved.shape[1] // width, add_solved, 0)

    @pl.when(has_after)
    def _():
        up.wait_send()
        down.wait_recv()

    @pl.when(has_before)
    def _():
        down.wait_send()
        up.wait_recv()


def arrivals(below, above):
    both = jnp.concatenate([below[...], above[...]], axis=1)
    species = both.shape[0] - 4
    w = both[species : species + 1, :]
    cell = both[species + 1 : species + 2, :].astype(I32) & 255
    return both[0:species, :], w, jnp.where(w > 0, cell, -1)


def mix_kernel(base, states, solved, cells, slots, below, above, sums, mixing, mixed, means, table, ready, sems):
    species, count = states.shape
    n_cells = sums.shape[1]
    width = count // MIX_PARTS
    x, w, cell = arrivals(below, above)
    acc = sums[...] + cell_sums(with_ones(x), w, cell, n_cells)
    acc = acc[0:ROWS] + acc[ROWS:]
    mean = acc[0:species] / acc[species : species + 1]
    means[...] = mean
    keep = jnp.exp(-MIX_RATE * mixing[...])
    table[...] = jnp.zeros_like(table)
    hi, lo = halves(mean * (1.0 - keep))
    table[0:species, 0:n_cells] = hi
    table[0:species, n_cells:] = lo
    hi, lo = halves(jnp.broadcast_to(keep, (16, n_cells)))
    table[ROWS:, 0:n_cells] = hi
    table[ROWS:, n_cells:] = lo

    def blend(x, cell):
        onehot = small_hot(cell, n_cells)
        pulled = nn(table[...], jnp.concatenate([onehot, onehot], axis=0))
        return x * pulled[ROWS : ROWS + 1] + pulled[:species]

    lane8 = iota((8, LANES), 1)
    per = count // LANES // 8

    def place(t):
        here = slice(t * LANES, (t + 1) * LANES)
        first = base[t, 0]
        inside = lane8 >= (first & 127)
        wanted = solved[ROWS + t // per : ROWS + t // per + 1, t % per * LANES : (t % per + 1) * LANES]
        wanted = jnp.broadcast_to(wanted.astype(I32), (8, LANES))
        picks = wanted & 127
        mine = wanted >= 0
        for g in range(ROWS // 8):
            n = min(8, species - 8 * g)
            rows = slice(8 * g, 8 * g + n)
            pair = jnp.where(inside[:n], solved[rows, tile_at(first >> 7)], solved[rows, tile_at((first >> 7) + 1)])
            ready[rows, here] = jnp.where(mine[:n], take(pair, picks[:n]), states[rows, here])

    sends = []
    for step in range(ready.shape[1] // width):
        at = slice(step * width, (step + 1) * width)
        if step < MIX_PARTS:
            for t in range(step * width // LANES, (step + 1) * width // LANES):
                place(t)
            x, cell = ready[:, at], jnp.where(slots[:, at] < 0, cells[:, at], -1)
        else:
            x, _, cell = arrivals(below, above)
            here = slice((step - MIX_PARTS) * width, (step - MIX_PARTS + 1) * width)
            x, cell = x[:, here], cell[:, here]
        ready[:, at] = blend(x, cell)
        sends.append(pltpu.make_async_copy(ready.at[:, at], mixed.at[:, at], sems.at[step]))
        sends[-1].start()
    for send in sends:
        send.wait()


def body(
    states, particle_mass, bin_index, cell_index, move_slot, react_list,
    rate_weights, stoichiometry, rate_scale, jacobian_inverse, mixing_rate, slot_count,
):
    species, count = states.shape
    n_cells = mixing_rate.shape[0]
    listed = react_list.shape[0]
    reactions = rate_scale.shape[0]
    n_bins = jacobian_inverse.shape[0]
    tiles = count // LANES
    wide = listed + 2 * LANES
    half = slot_count // 2
    square = lambda a: a.reshape(tiles, LANES)
    line = lambda a: a.reshape(1, -1)
    small = [
        square(move_slot), line(react_list), square(particle_mass), square(bin_index), square(cell_index),
        line(rate_scale), rate_weights.T, stoichiometry, jnp.transpose(jacobian_inverse, (1, 0, 2)),
    ]
    lower, upper, base, solved, held = pl.pallas_call(
        react_kernel,
        in_specs=[pl.BlockSpec(memory_space=pltpu.HBM)] * (1 + SMALL),
        out_shape=(
            pltpu.VMEM((ROWS, half), F32),
            pltpu.VMEM((ROWS, half), F32),
            pltpu.VMEM((tiles, LANES), I32),
            pltpu.VMEM((ROWS + 8, wide), F32),
            pltpu.VMEM((species, count), F32),
        ),
        scratch_shapes=[pltpu.VMEM(a.shape, a.dtype) for a in small] + [
            pltpu.SMEM((tiles, LANES), I32),
            pltpu.VMEM((tiles, LANES), I32),
            pltpu.VMEM((8, count), F32),
            pltpu.VMEM((ROWS, LANES), F32),
            pltpu.VMEM((tiles * 8, 2 * LANES), I32),
            pltpu.VMEM((2, tiles, LANES), I32),
            pltpu.VMEM((ROWS, n_bins * ROWS), BF16),
            pltpu.VMEM((reactions, ROWS), BF16),
            pltpu.VMEM((ROWS, reactions), BF16),
            pltpu.VMEM((reactions, LANES), F32),
            pltpu.VMEM((ROWS, slot_count + 2 * LANES), F32),
            pltpu.VMEM((2 * ROWS, slot_count), BF16),
            pltpu.SemaphoreType.DMA,
            pltpu.SemaphoreType.DMA((LOADS,)),
            pltpu.SemaphoreType.DMA((SMALL,)),
        ],
        compiler_params=pltpu.CompilerParams(vmem_limit_bytes=54 * 2**20),
        name="react",
    )(states, *small)
    devices = lax.axis_size("dev")
    masses, cell_line, slot_line = line(particle_mass), line(cell_index), line(move_slot)
    vmem = pl.BlockSpec(memory_space=pltpu.VMEM)
    sums, below, above = pl.pallas_call(
        functools.partial(exchange_kernel, devices),
        in_specs=[vmem] * 8,
        out_shape=(
            pltpu.VMEM((2 * ROWS, n_cells), F32),
            pltpu.VMEM((ROWS, half), F32),
            pltpu.VMEM((ROWS, half), F32),
        ),
        scratch_shapes=[pltpu.SemaphoreType.DMA((2,)), pltpu.SemaphoreType.DMA((2,))],
        compiler_params=pltpu.CompilerParams(
            vmem_limit_bytes=32 * 2**20, collective_id=0, has_side_effects=True
        ),
        cost_estimate=pl.CostEstimate(
            flops=4 * ROWS * count * n_cells, bytes_accessed=8 * species * count, transcendentals=0
        ),
        name="exchange",
    )(base, held, solved, masses, cell_line, slot_line, lower, upper)
    mixed, means = pl.pallas_call(
        mix_kernel,
        in_specs=[pl.BlockSpec(memory_space=pltpu.SMEM)] + [vmem] * 8,
        out_specs=(pl.BlockSpec(memory_space=pl.ANY), vmem),
        out_shape=(
            jax.ShapeDtypeStruct((species, count + slot_count), F32),
            jax.ShapeDtypeStruct((species, n_cells), F32),
        ),
        scratch_shapes=[
            pltpu.VMEM((ROWS + 16, 2 * n_cells), BF16),
            pltpu.VMEM((species, count + slot_count), F32),
            pltpu.SemaphoreType.DMA(((count + slot_count) * MIX_PARTS // count,)),
        ],
        compiler_params=pltpu.CompilerParams(vmem_limit_bytes=32 * 2**20),
        name="mix",
    )(base, held, solved, cell_line, slot_line, below, above, sums, line(mixing_rate))
    return mixed, means


MCAP = 512


def solution(mesh):
    each, all_of = P("dev"), P()
    return jax.shard_map(
        functools.partial(body, slot_count=2 * MCAP),
        mesh=mesh,
        in_specs=(P(None, "dev"), each, each, each, each, each, all_of, all_of, all_of, all_of, each),
        out_specs=(P(None, "dev"), P(None, "dev")),
        check_vma=False,
    )
```

```python
import functools
import math
import jax
import jax.numpy as jnp
from jax import lax
from jax.experimental import pallas as pl
from jax.experimental.pallas import tpu as pltpu
from jax.sharding import PartitionSpec as P

NEWTON = 3
CHEM_STEP = 0.5
MIX_RATE = 0.5
LANES = 128
SUB = 512
SUBS = 2
NCOL = SUB * SUBS
CHUNK = 256
LAG = 2
ROWS = 192
UNROLL = 8
LOADS = 4
SMALL = 9
EARLY = 2
MIX_PARTS = 16
F32, BF16, I32 = jnp.float32, jnp.bfloat16, jnp.int32


def nt(a, b):
    return lax.dot_general(a, b, (((1,), (1,)), ((), ())), preferred_element_type=F32)


def nn(a, b):
    return jnp.dot(a, b, preferred_element_type=F32)


def iota(shape, dim):
    return lax.broadcasted_iota(I32, shape, dim)


def halves(x):
    hi = x.astype(BF16)
    return hi, (x - hi.astype(F32)).astype(BF16)


def hot(row, size):
    return (iota((size, row.shape[1]), 0) == row).astype(F32).astype(BF16)


def small_hot(row, size):
    which = iota((size, row.shape[1]), 0).astype(F32).astype(BF16)
    return jnp.where(which == row.astype(F32).astype(BF16), BF16(1), BF16(0))


def take(x, index):
    return jnp.take_along_axis(x, index, axis=1, mode="promise_in_bounds")


def tile_at(t, count=1):
    return pl.ds(pl.multiple_of(t * LANES, LANES), count * LANES)


def ranks(mask):
    tiles = mask.shape[0]
    upper_tri = (iota((LANES, LANES), 0) < iota((LANES, LANES), 1)).astype(F32).astype(BF16)
    lower_tri = (iota((tiles, tiles), 1) < iota((tiles, tiles), 0)).astype(F32).astype(BF16)
    half = mask.astype(BF16)
    before = jnp.sum(nn(lower_tri, half), axis=1, keepdims=True)
    return (nn(half, upper_tri) + before).astype(I32), before


def total_of(x):
    return jnp.sum(jnp.sum(x, axis=0, keepdims=True), axis=1, keepdims=True)


def react_kernel(
    states, *refs,
):
    small, refs = refs[:SMALL], refs[SMALL:]
    lower, upper, base_v, solved, st, *refs = refs
    held, refs = refs[:SMALL], refs[SMALL:]
    slots, rlist, mass, bins, cells, scale_row, rate_wt, stoich, jac3 = held
    (base_s, rank, tail, partial, index, low_rank, jac, rate_w, stoich_w, scale, packed, stack, sem, load_sems, small_sems) = refs
    species, count = states.shape
    tiles = count // LANES
    half = lower.shape[1]
    moved_tiles = 2 * half // LANES
    most = rlist.shape[1]
    groups = ROWS // 8
    part = count // LOADS
    loads = [
        pltpu.make_async_copy(
            states.at[:, pl.ds(i * part, part)], st.at[:, pl.ds(i * part, part)], load_sems.at[i]
        )
        for i in range(LOADS)
    ]
    fetches = [pltpu.make_async_copy(small[i], held[i], small_sems.at[i]) for i in range(SMALL)]
    for copy in fetches[:EARLY] + loads + fetches[EARLY:]:
        copy.start()
    for copy in fetches[:EARLY]:
        copy.wait()

    r = rlist[...]
    listed = nt(hot(r >> 7, tiles), hot(r & 127, LANES))
    total = total_of(listed)
    moving = (slots[...] >= 0).astype(F32)
    total_move = total_of(moving)
    place, before = ranks(listed)
    place_move, before_move = ranks(moving)
    rank[...] = jnp.where(listed > 0, place, -1)
    lane = iota((tiles, LANES), 1)
    row = iota((tiles, LANES), 0)
    table = jnp.where(lane == 0, before, jnp.where(lane == 1, total, jnp.where(lane == 2, total_move, before_move)))
    for q in range(moved_tiles + 1):
        first = jnp.where((moving > 0) & (place_move == q * LANES), place.astype(F32) - total, 0.0)
        table = jnp.where((lane == 4) & (row == q), total_of(first) + total, table)
    base_v[...] = table.astype(I32)
    bases = pltpu.make_async_copy(base_v, base_s, sem)
    bases.start()
    low_rank[0] = jnp.where(listed > 0, place & 127, -1)
    low_rank[1] = jnp.where(moving > 0, place_move & 127, -1)

    for copy in fetches[EARLY:]:
        copy.wait()
    scale[...] = jnp.transpose(jnp.broadcast_to(scale_row[...], (LANES, scale_row.shape[1])))
    rate_w[...] = jnp.zeros_like(rate_w)
    rate_w[:, 0:species] = jnp.transpose(rate_wt[...].astype(F32)).astype(BF16)
    stoich_w[...] = jnp.zeros_like(stoich_w)
    stoich_w[0:species, :] = stoich[...]
    jac[...] = jnp.zeros_like(jac)
    for b in range(jac3.shape[1]):
        jac[0:species, b * ROWS : b * ROWS + species] = jac3[:, b, :]

    lanes8 = iota((8, LANES), 1).astype(F32).astype(BF16)

    def inverses(k, c):
        for u in range(UNROLL):
            t = k * UNROLL + u
            onehots = jnp.concatenate([small_hot(low_rank[s, pl.ds(t, 1), :], LANES) for s in range(2)], axis=0)
            at = pl.ds(pl.multiple_of(t * 8, 8), 8)
            index[at, :] = nt(lanes8, onehots).astype(I32)
        return c

    inverses(0, 0)
    bases.wait()
    for load in loads:
        load.wait()
    rest = species - (groups - 1) * 8
    for t in range(tiles):
        at = slice(t * LANES, (t + 1) * LANES)
        rows = [mass[t : t + 1, :], (cells[t : t + 1, :] + 256 * bins[t : t + 1, :]).astype(F32),
                slots[t : t + 1, :].astype(F32), rank[t : t + 1, :].astype(F32)]
        per = tiles // 8
        solved[ROWS + t // per : ROWS + t // per + 1, t % per * LANES : (t % per + 1) * LANES] = rows[3]
        tail[0:rest, at] = st[(groups - 1) * 8 : species, at]
        for i, value in enumerate(rows):
            tail[rest + i : rest + i + 1, at] = value

    lane8 = iota((8, LANES), 1)

    def source(g, t):
        if g == groups - 1:
            return tail[:, tile_at(t)]
        return st[8 * g : 8 * g + 8, tile_at(t)]

    def compact_tile(out, column, which, total_at, t, carry):
        first = base_s[t, column]
        after = jnp.where(t == tiles - 1, base_s[0, total_at], base_s[jnp.minimum(t + 1, tiles - 1), column])
        wraps = (after >> 7) != (first >> 7)
        inside = lane8 >= (first & 127)
        picks = index[pl.ds(pl.multiple_of(t * 8, 8), 8), which * LANES : (which + 1) * LANES]
        at = tile_at(first >> 7)
        fresh = []
        for g in range(groups):
            got = take(source(g, t), picks)
            new = jnp.where(inside, got, carry[g])
            out[8 * g : 8 * g + 8, at] = new
            fresh.append(jnp.where(wraps, got, new))
        return tuple(fresh)

    def compact(out, column, which, total_at, begin, carry, beside):
        def some(k, carry):
            for u in range(UNROLL):
                carry = compact_tile(out, column, which, total_at, k * UNROLL + u, carry)
            beside(k)
            return carry

        carry = lax.fori_loop(begin, tiles // UNROLL, some, carry)
        at = tile_at(base_s[0, total_at] >> 7)
        for g in range(groups):
            out[8 * g : 8 * g + 8, at] = carry[g]

    empty = tuple(jnp.zeros((8, LANES), F32) for _ in range(groups))
    following = lambda k: inverses(jnp.minimum(k + 1, tiles // UNROLL - 1), 0)
    compact(solved, 0, 0, 1, 0, empty, following)
    partial[...] = jnp.zeros_like(partial)
    load_partial = lambda: tuple(partial[8 * g : 8 * g + 8, :] for g in range(groups))
    beside_step = tiles * NCOL // most

    reactions = rate_w.shape[0]
    chunks = [(lo, min(CHUNK, reactions - lo)) for lo in range(0, reactions, CHUNK)]

    def solve(k, c):
        subs = []
        for s in range(SUBS):
            at = pl.ds(pl.multiple_of((k * SUBS + s) * SUB, SUB), SUB)
            level = (solved[species + 1 : species + 2, at].astype(I32) >> 8).astype(F32)
            subs.append({"at": at, "start": solved[0:ROWS, at], "level": level, "d": None})
        waiting = []
        finishes = NEWTON * SUBS * len(chunks)
        moved = {"carry": load_partial(), "done": 0, "finished": 0}

        def move_some():
            moved["finished"] += 1
            while moved["done"] * finishes < beside_step * moved["finished"]:
                t = k * beside_step + moved["done"]
                moved["carry"] = compact_tile(packed, 3, 1, 2, t, moved["carry"])
                moved["done"] += 1

        def finish():
            sub, i, u = waiting.pop(0)
            lo, size = chunks[i]
            soft = jnp.maximum(u, jnp.log(1.0 + jnp.exp(jnp.minimum(u, 87.0))))
            rate = (soft * scale[lo : lo + size, 0:1]).astype(BF16)
            term = nn(stoich_w[:, lo : lo + size], rate)
            sub["source"] = term if i == 0 else sub["source"] + term
            if i == len(chunks) - 1:
                d = sub["d"]
                residual = -CHEM_STEP * sub["source"]
                residual = (residual if d is None else d + residual).astype(BF16)
                masked = jnp.concatenate(
                    [jnp.where(sub["level"] == b, residual, BF16(0)) for b in range(jac3.shape[1])], axis=0
                )
                update = nn(jac[...], masked)
                sub["d"] = -update if d is None else d - update

        for sweep in range(NEWTON):
            for sub in subs:
                x = None
                for i, (lo, size) in enumerate(chunks):
                    if x is None:
                        x = (sub["start"] if sub["d"] is None else sub["start"] + sub["d"]).astype(BF16)
                    waiting.append((sub, i, nn(rate_w[lo : lo + size, :], x)))
                    if len(waiting) > LAG:
                        finish()
                        move_some()
        while waiting:
            finish()
            move_some()
        for g in range(groups):
            partial[8 * g : 8 * g + 8, :] = moved["carry"][g]
        for sub in subs:
            solved[0:ROWS, sub["at"]] = sub["start"] + sub["d"]
        return c

    steps = (base_s[0, 1] + NCOL - 1) // NCOL
    lax.fori_loop(0, steps, solve, 0)
    compact(packed, 3, 1, 2, steps * (beside_step // UNROLL), load_partial(), lambda k: None)

    spans = []
    for q in range(moved_tiles):
        low, high = base_s[q, 4], base_s[q + 1, 4]
        spans.append((low >> 7, ((high - 1) >> 7) - (low >> 7) + 1))
    longest = functools.reduce(jnp.maximum, [s[1] for s in spans])
    final = most // LANES - 1

    def expand(s, c):
        for q in range(moved_tiles):
            here = slice(q * LANES, (q + 1) * LANES)
            t = jnp.minimum(spans[q][0] + s, final)
            wanted = packed[ROWS - 1 : ROWS, here].astype(I32)
            wanted = jnp.broadcast_to(jnp.where(lane8[0:1] + q * LANES < base_s[0, 2], wanted, -1), (8, LANES))
            mine = (wanted >> 7) == t
            picks = wanted & 127
            for g in range(groups):
                rows = slice(8 * g, 8 * g + 8)
                keep = mine if g < groups - 1 else mine & (iota((8, LANES), 0) < rest)
                packed[rows, here] = jnp.where(keep, take(solved[rows, tile_at(t)], picks), packed[rows, here])
        return c

    lax.fori_loop(0, longest, expand, 0)

    mine = packed[:, 0 : 2 * half]
    filled = iota((1, 2 * half), 1) < base_s[0, 2]
    mine = jnp.where(filled, mine, 0.0)
    hi, lo = halves(mine)
    stack[0:ROWS, :] = hi
    stack[ROWS:, :] = lo
    slot = jnp.where(filled, mine[species + 2 : species + 3].astype(I32), -1)
    for out, first in ((lower, 0), (upper, half)):
        moved = nt(stack[...], hot_rows(slot - first, half))
        out[...] = moved[0:ROWS] + moved[ROWS:]


def hot_rows(row, size):
    return (iota((size, row.shape[1]), 0) == row).astype(F32).astype(BF16)


def cell_sums(x, w, cell, n_cells):
    hi, lo = halves(x * w)
    onehot = small_hot(cell, n_cells)
    return nt(jnp.concatenate([hi, lo], axis=0), onehot)


def with_ones(x):
    width = x.shape[1]
    return jnp.concatenate([x, jnp.ones((1, width), F32), jnp.zeros((ROWS - x.shape[0] - 1, width), F32)], axis=0)


def exchange_kernel(
    devices, base, states, solved, mass, cells, slots, lower, upper, sums, below, above, sent, got,
):
    me = lax.axis_index("dev")
    after, before = lax.rem(me + 1, devices), lax.rem(me + devices - 1, devices)
    has_after, has_before = me < devices - 1, me > 0
    barrier = pltpu.get_barrier_semaphore()
    for there, other in ((has_after, after), (has_before, before)):
        @pl.when(there)
        def _(other=other):
            pl.semaphore_signal(barrier, inc=1, device_id=(other,), device_id_type=pl.DeviceIdType.MESH)
    inner = has_after & has_before

    @pl.when(inner)
    def _():
        pl.semaphore_wait(barrier, 2)

    @pl.when(jnp.logical_not(inner))
    def _():
        pl.semaphore_wait(barrier, 1)

    def transfer(i, src, dst, other):
        return pltpu.make_async_remote_copy(
            src_ref=src, dst_ref=dst, send_sem=sent.at[i], recv_sem=got.at[i],
            device_id=(other,), device_id_type=pl.DeviceIdType.MESH,
        )

    up, down = transfer(0, upper, below, after), transfer(1, lower, above, before)

    @pl.when(has_after)
    def _():
        up.start()

    @pl.when(has_before)
    def _():
        down.start()

    @pl.when(me == 0)
    def _():
        below[...] = jnp.zeros_like(below)

    @pl.when(me == devices - 1)
    def _():
        above[...] = jnp.zeros_like(above)

    species, count = states.shape
    per = count // LANES // 8
    width = per * LANES
    total = base[0:1, 1:2]

    def add(step, c):
        at = tile_at(step * per, per)
        rank = jnp.where(iota((8, width), 0) == step, solved[ROWS : ROWS + 8, 0:width], 0.0)
        idle = (slots[:, at] < 0) & (jnp.sum(rank, axis=0, keepdims=True) < 0)
        w = jnp.where(idle, mass[:, at], 0.0)
        sums[...] += cell_sums(with_ones(states[:, at]), w, cells[:, at], sums.shape[1])
        return c

    def add_solved(step, c):
        at = tile_at(step * per, per)
        valid = iota((1, width), 1) + step * width < total
        x = jnp.where(valid, solved[0:ROWS, at], 0.0)
        w = jnp.where(valid & (x[species + 2 : species + 3] < 0), x[species : species + 1], 0.0)
        cell = x[species + 1 : species + 2].astype(I32) & 255
        sums[...] += cell_sums(with_ones(x[0:species]), w, cell, sums.shape[1])
        return c

    sums[...] = jnp.zeros_like(sums)
    lax.fori_loop(0, 8, add, 0)
    lax.fori_loop(0, solved.shape[1] // width, add_solved, 0)

    @pl.when(has_after)
    def _():
        up.wait_send()
        down.wait_recv()

    @pl.when(has_before)
    def _():
        down.wait_send()
        up.wait_recv()


def arrivals(below, above):
    both = jnp.concatenate([below[...], above[...]], axis=1)
    species = both.shape[0] - 4
    w = both[species : species + 1, :]
    cell = both[species + 1 : species + 2, :].astype(I32) & 255
    return both[0:species, :], w, jnp.where(w > 0, cell, -1)


def mix_kernel(base, states, solved, cells, slots, below, above, sums, mixing, mixed, means, table, ready, base_s, base_sem, sems):
    species, count = states.shape
    bases = pltpu.make_async_copy(base, base_s, base_sem)
    bases.start()
    n_cells = sums.shape[1]
    width = count // MIX_PARTS
    x, w, cell = arrivals(below, above)
    acc = sums[...] + cell_sums(with_ones(x), w, cell, n_cells)
    acc = acc[0:ROWS] + acc[ROWS:]
    mean = acc[0:species] / acc[species : species + 1]
    means[...] = mean
    keep = jnp.exp(-MIX_RATE * mixing[...])
    table[...] = jnp.zeros_like(table)
    hi, lo = halves(mean * (1.0 - keep))
    table[0:species, 0:n_cells] = hi
    table[0:species, n_cells:] = lo
    hi, lo = halves(jnp.broadcast_to(keep, (16, n_cells)))
    table[ROWS:, 0:n_cells] = hi
    table[ROWS:, n_cells:] = lo

    def blend(x, cell):
        onehot = small_hot(cell, n_cells)
        pulled = nn(table[...], jnp.concatenate([onehot, onehot], axis=0))
        return x * pulled[ROWS : ROWS + 1] + pulled[:species]

    lane8 = iota((8, LANES), 1)
    per = count // LANES // 8

    def place(t):
        here = slice(t * LANES, (t + 1) * LANES)
        first = base_s[t, 0]
        inside = lane8 >= (first & 127)
        wanted = solved[ROWS + t // per : ROWS + t // per + 1, t % per * LANES : (t % per + 1) * LANES]
        wanted = jnp.broadcast_to(wanted.astype(I32), (8, LANES))
        picks = wanted & 127
        mine = wanted >= 0
        for g in range(ROWS // 8):
            n = min(8, species - 8 * g)
            rows = slice(8 * g, 8 * g + n)
            pair = jnp.where(inside[:n], solved[rows, tile_at(first >> 7)], solved[rows, tile_at((first >> 7) + 1)])
            ready[rows, here] = jnp.where(mine[:n], take(pair, picks[:n]), states[rows, here])

    bases.wait()
    sends = []
    for step in range(ready.shape[1] // width):
        at = slice(step * width, (step + 1) * width)
        if step < MIX_PARTS:
            for t in range(step * width // LANES, (step + 1) * width // LANES):
                place(t)
            x, cell = ready[:, at], jnp.where(slots[:, at] < 0, cells[:, at], -1)
        else:
            x, _, cell = arrivals(below, above)
            here = slice((step - MIX_PARTS) * width, (step - MIX_PARTS + 1) * width)
            x, cell = x[:, here], cell[:, here]
        ready[:, at] = blend(x, cell)
        sends.append(pltpu.make_async_copy(ready.at[:, at], mixed.at[:, at], sems.at[step]))
        sends[-1].start()
    for send in sends:
        send.wait()


def body(
    states, particle_mass, bin_index, cell_index, move_slot, react_list,
    rate_weights, stoichiometry, rate_scale, jacobian_inverse, mixing_rate, slot_count,
):
    species, count = states.shape
    n_cells = mixing_rate.shape[0]
    listed = react_list.shape[0]
    reactions = rate_scale.shape[0]
    n_bins = jacobian_inverse.shape[0]
    tiles = count // LANES
    wide = listed + 2 * LANES
    half = slot_count // 2
    square = lambda a: a.reshape(tiles, LANES)
    line = lambda a: a.reshape(1, -1)
    small = [
        square(move_slot), line(react_list), square(particle_mass), square(bin_index), square(cell_index),
        line(rate_scale), rate_weights.T, stoichiometry, jnp.transpose(jacobian_inverse, (1, 0, 2)),
    ]
    lower, upper, base, solved, held = pl.pallas_call(
        react_kernel,
        in_specs=[pl.BlockSpec(memory_space=pltpu.HBM)] * (1 + SMALL),
        out_shape=(
            pltpu.VMEM((ROWS, half), F32),
            pltpu.VMEM((ROWS, half), F32),
            pltpu.VMEM((tiles, LANES), I32),
            pltpu.VMEM((ROWS + 8, wide), F32),
            pltpu.VMEM((species, count), F32),
        ),
        scratch_shapes=[pltpu.VMEM(a.shape, a.dtype) for a in small] + [
            pltpu.SMEM((tiles, LANES), I32),
            pltpu.VMEM((tiles, LANES), I32),
            pltpu.VMEM((8, count), F32),
            pltpu.VMEM((ROWS, LANES), F32),
            pltpu.VMEM((tiles * 8, 2 * LANES), I32),
            pltpu.VMEM((2, tiles, LANES), I32),
            pltpu.VMEM((ROWS, n_bins * ROWS), BF16),
            pltpu.VMEM((reactions, ROWS), BF16),
            pltpu.VMEM((ROWS, reactions), BF16),
            pltpu.VMEM((reactions, LANES), F32),
            pltpu.VMEM((ROWS, slot_count + 2 * LANES), F32),
            pltpu.VMEM((2 * ROWS, slot_count), BF16),
            pltpu.SemaphoreType.DMA,
            pltpu.SemaphoreType.DMA((LOADS,)),
            pltpu.SemaphoreType.DMA((SMALL,)),
        ],
        compiler_params=pltpu.CompilerParams(vmem_limit_bytes=54 * 2**20),
        name="react",
    )(states, *small)
    devices = lax.axis_size("dev")
    masses, cell_line, slot_line = line(particle_mass), line(cell_index), line(move_slot)
    vmem = pl.BlockSpec(memory_space=pltpu.VMEM)
    sums, below, above = pl.pallas_call(
        functools.partial(exchange_kernel, devices),
        in_specs=[vmem] * 8,
        out_shape=(
            pltpu.VMEM((2 * ROWS, n_cells), F32),
            pltpu.VMEM((ROWS, half), F32),
            pltpu.VMEM((ROWS, half), F32),
        ),
        scratch_shapes=[pltpu.SemaphoreType.DMA((2,)), pltpu.SemaphoreType.DMA((2,))],
        compiler_params=pltpu.CompilerParams(
            vmem_limit_bytes=32 * 2**20, collective_id=0, has_side_effects=True
        ),
        cost_estimate=pl.CostEstimate(
            flops=4 * ROWS * count * n_cells, bytes_accessed=8 * species * count, transcendentals=0
        ),
        name="exchange",
    )(base, held, solved, masses, cell_line, slot_line, lower, upper)
    mixed, means = pl.pallas_call(
        mix_kernel,
        in_specs=[vmem] * 9,
        out_specs=(pl.BlockSpec(memory_space=pl.ANY), vmem),
        out_shape=(
            jax.ShapeDtypeStruct((species, count + slot_count), F32),
            jax.ShapeDtypeStruct((species, n_cells), F32),
        ),
        scratch_shapes=[
            pltpu.VMEM((ROWS + 16, 2 * n_cells), BF16),
            pltpu.VMEM((species, count + slot_count), F32),
            pltpu.SMEM((tiles, LANES), I32),
            pltpu.SemaphoreType.DMA,
            pltpu.SemaphoreType.DMA(((count + slot_count) * MIX_PARTS // count,)),
        ],
        compiler_params=pltpu.CompilerParams(vmem_limit_bytes=32 * 2**20),
        name="mix",
    )(base, held, solved, cell_line, slot_line, below, above, sums, line(mixing_rate))
    return mixed, means


MCAP = 512


def solution(mesh):
    each, all_of = P("dev"), P()
    return jax.shard_map(
        functools.partial(body, slot_count=2 * MCAP),
        mesh=mesh,
        in_specs=(P(None, "dev"), each, each, each, each, each, all_of, all_of, all_of, all_of, each),
        out_specs=(P(None, "dev"), P(None, "dev")),
        check_vma=False,
    )
```
